32 devices in a mesh: parts: 2 (over y), replica: 4 (over x, core), tensor: 4 (over z).
Axes of the slice: x: 2, y: 2, z: 4, core: 2. Of those that a mesh axis runs over, the one named last changes fastest.
Arguments:
- act_codes: bfloat16 [256, 8192], P(('parts', 'replica'), 'tensor'), parts along dimension 0, may hold values from -128 to 127, as said below
- act_scale: float32 [256], P('parts'), parts along dimension 0, may hold values from 0.006 to 0.02
- adapter_ids: int32 [256], P(('parts', 'replica')), parts along dimension 0, may hold values from 0 to 7, as said below
- seg_starts: int32 [8, 4], P('parts'), parts along dimension 0, may hold values from 0 to 32, as said below
- pool_index: int32 [16], P('parts'), parts along dimension 0, may hold values from 0 to 7, as said below
- gate_levels: bfloat16 [8192, 32768], P(None, ('replica', 'tensor')), may hold values from -8 to 7, as said below
- gate_scale: float32 [64, 32768], P(None, ('replica', 'tensor')), may hold values from 0.0008 to 0.0035
- up_levels: bfloat16 [8192, 32768], P(None, ('replica', 'tensor')), may hold values from -8 to 7, as said below
- up_scale: float32 [64, 32768], P(None, ('replica', 'tensor')), may hold values from 0.0008 to 0.0035
- down_levels: bfloat16 [32768, 8192], P(('replica', 'tensor')), may hold values from -8 to 7, as said below
- down_scale: float32 [256, 8192], P(('replica', 'tensor')), may hold values from 0.0006 to 0.0024
- shrink_weight: bfloat16 [32768, 512], P(('replica', 'tensor')), may hold values from -0.03125 to 0.03125
- expand_matrix_rows: bfloat16 [8, 64, 8192], P('replica', None, 'tensor'), may hold values from -1.5 to 1.5
Outputs:
- mixed: bfloat16 [256, 8192], P(('parts', 'replica'), 'tensor'), parts along dimension 0
The draws below stay inside these ranges and needn't reach their ends.
There are 2 independent parts, one for each index of `parts`. The reference program is written for one: setup_inputs(seed, part) draws one part's arguments, and reference() takes and returns one part's arrays. A program takes and returns all parts, laid end to end along the dimension named above; an argument that names none is the same for every part. Nothing has to cross between parts.
Inputs may be any that keep to these rules, and one draw needn't show every extreme that they name: `act_codes`: whole numbers. `gate_levels`: whole numbers. `up_levels`: whole numbers. `down_levels`: whole numbers. `pool_index`: each adapter's pool row; every pool row is used once. Pool rows a * 2 to a * 2 + 1 are held by replica a. `seg_starts`: row r starts with 0 and rises strictly over its live slots; the unused slots after them hold 32. Some replica uses all 4 slots. The segments of one replica name distinct adapters, at most 1 of them held by any one replica; some replica takes exactly 1 from every replica. `adapter_ids`: equal within each segment of a replica.
All inputs are finite; a program needn't handle non-finite values.
Results may differ from the reference program's by a relative error of at most 0.0095.
Values may be sent and summed in bfloat16 or wider, within the bound.
No kernel may reach another device: no remote copies, remote signals or barrier semaphores. Data moves between devices by JAX's collectives and lax.ppermute only.
A program may use at most 384 MiB of HBM per device.

```python
import math
import jax
import jax.numpy as jnp
from jax import lax

MODEL_WIDTH = 8192
FF = 32768
ADAPTER_RANK = 64
GROUP = 128
ROWS_DEV = 32
ADP_DEV = 2
CAP = 1
REPLICAS = 4
SLOTS = 4
ADAPTER_COUNT = 8
ROWS_ALL = 128


def draw_tables(key):
    keys = jax.random.split(key, 6)
    pool_rows = jax.random.permutation(keys[0], ADAPTER_COUNT).astype(jnp.int32)
    holder = jnp.argsort(pool_rows).astype(jnp.int32)
    live = jax.random.randint(keys[1], (REPLICAS,), 1, SLOTS // 2 + 1, dtype=jnp.int32)
    busiest = jax.random.randint(keys[2], (), 0, REPLICAS, dtype=jnp.int32)
    live = jnp.where(jnp.arange(REPLICAS, dtype=jnp.int32) == busiest, SLOTS, live)
    pick_keys = jax.random.split(keys[3], REPLICAS * REPLICAS)
    picks = jax.vmap(lambda subkey: jax.random.permutation(subkey, ADP_DEV)[:CAP])(pick_keys).astype(jnp.int32)
    picks = picks.reshape(REPLICAS, REPLICAS, CAP) + (jnp.arange(REPLICAS, dtype=jnp.int32) * ADP_DEV)[None, :, None]
    picks = picks.reshape(REPLICAS, SLOTS)
    order_keys = jax.random.split(keys[4], REPLICAS)
    shuffled = jax.vmap(lambda subkey, chosen: jax.random.permutation(subkey, chosen))(order_keys, picks)
    slot_adapter = holder[shuffled]
    cut_keys = jax.random.split(keys[5], REPLICAS)
    cuts = jax.vmap(lambda subkey: jax.random.permutation(subkey, ROWS_DEV - 1))(cut_keys).astype(jnp.int32) + 1
    cuts = jnp.where(jnp.arange(ROWS_DEV - 1, dtype=jnp.int32)[None, :] < live[:, None] - 1, cuts, ROWS_DEV)
    cuts = jnp.sort(cuts, axis=1)[:, :SLOTS - 1]
    starts = jnp.concatenate([jnp.zeros((REPLICAS, 1), jnp.int32), cuts], axis=1).astype(jnp.int32)
    positions = jnp.arange(ROWS_DEV, dtype=jnp.int32)
    row_slot = jnp.sum((starts[:, None, 1:] <= positions[None, :, None]).astype(jnp.int32), axis=2)
    row_ids = jnp.take_along_axis(slot_adapter, row_slot, axis=1).reshape(ROWS_ALL).astype(jnp.int32)
    return (pool_rows, starts, row_ids)


def draw_pool_index(key, part):
    return draw_tables(key)[0]


def draw_seg_starts(key, part):
    return draw_tables(key)[1]


def draw_adapter_ids(key, part):
    return draw_tables(key)[2]


def draw_act_codes(key, part):
    key = jax.random.fold_in(key, 11)
    whole = jax.random.randint(key, (ROWS_ALL, MODEL_WIDTH), -128, 128, dtype=jnp.int32)
    return whole.astype(jnp.float32).astype(jnp.bfloat16)


def draw_gate_levels(key, part):
    key = jax.random.fold_in(key, 12)
    whole = jax.random.randint(key, (MODEL_WIDTH, FF), -8, 8, dtype=jnp.int32)
    return whole.astype(jnp.float32).astype(jnp.bfloat16)


def draw_up_levels(key, part):
    key = jax.random.fold_in(key, 13)
    whole = jax.random.randint(key, (MODEL_WIDTH, FF), -8, 8, dtype=jnp.int32)
    return whole.astype(jnp.float32).astype(jnp.bfloat16)


def draw_down_levels(key, part):
    key = jax.random.fold_in(key, 14)
    whole = jax.random.randint(key, (FF, MODEL_WIDTH), -8, 8, dtype=jnp.int32)
    return whole.astype(jnp.float32).astype(jnp.bfloat16)


def block_scale(own_key, shape, cuts, smallest, high):
    level, own = 1.0, jax.random.fold_in(own_key, 6)
    for position, blocks in cuts:
        steps = jnp.exp(jax.random.uniform(jax.random.fold_in(own, position), (blocks,), jnp.float32, smallest / len(cuts), high / len(cuts)))
        level = level * jnp.repeat(steps, shape[position] // blocks).reshape([-1 if axis == position else 1 for axis in range(len(shape))])
    return level


def centred(key, shape, scale, limit, shards=(), held_as=jnp.bfloat16):
    values = scale * jax.random.normal(key, shape, jnp.float32)
    if shards:
        values = values * block_scale(key, shape, shards, -0.22, 0.18)
    return jnp.clip(values, -limit, limit).astype(held_as)


def setup_inputs(seed: int = 0, part: int = 0) -> dict:
    seeds = jax.random.split(jax.random.key(seed), 14)
    own_keys = jax.random.split(jax.random.fold_in(seeds[13], part), 14)
    act_codes = draw_act_codes(jax.random.fold_in(jax.random.fold_in(seeds[13], part), 71), part)
    act_scale = jnp.clip(jnp.exp(jax.random.uniform(own_keys[1], (ROWS_ALL,), jnp.float32, math.log(0.006), math.log(0.02))), 0.006, 0.02)
    adapter_ids = draw_adapter_ids(jax.random.fold_in(jax.random.fold_in(seeds[13], part), 71), part)
    seg_starts = draw_seg_starts(jax.random.fold_in(jax.random.fold_in(seeds[13], part), 71), part)
    pool_index = draw_pool_index(jax.random.fold_in(jax.random.fold_in(seeds[13], part), 71), part)
    gate_levels = draw_gate_levels(jax.random.fold_in(seeds[13], 71), part)
    gate_scale = jnp.clip(jnp.exp(math.log(0.0035) - 1.4759066 * jax.random.uniform(seeds[6], (MODEL_WIDTH // GROUP, FF), jnp.float32) ** block_scale(seeds[6], (MODEL_WIDTH // GROUP, FF), ((1, 16),), -0.2, 0.2)), 0.0008, 0.0035)
    up_levels = draw_up_levels(jax.random.fold_in(seeds[13], 71), part)
    up_scale = jnp.clip(jnp.exp(math.log(0.0035) - 1.4759066 * jax.random.uniform(seeds[8], (MODEL_WIDTH // GROUP, FF), jnp.float32) ** block_scale(seeds[8], (MODEL_WIDTH // GROUP, FF), ((1, 16),), -0.2, 0.2)), 0.0008, 0.0035)
    down_levels = draw_down_levels(jax.random.fold_in(seeds[13], 71), part)
    down_scale = jnp.clip(jnp.exp(math.log(0.0024) - 1.3862944 * jax.random.uniform(seeds[10], (FF // GROUP, MODEL_WIDTH), jnp.float32) ** block_scale(seeds[10], (FF // GROUP, MODEL_WIDTH), ((0, 16),), -0.2, 0.2)), 0.0006, 0.0024)
    shrink_weight = centred(seeds[11], (FF, ADAPTER_COUNT * ADAPTER_RANK), FF ** -0.5, 0.03125, ((0, 16),))
    expand_matrix_rows = centred(seeds[12], (ADAPTER_COUNT, ADAPTER_RANK, MODEL_WIDTH), 16 ** -0.5, 1.5, ((0, 4), (2, 4)))
    return dict(act_codes=act_codes, act_scale=act_scale, adapter_ids=adapter_ids, seg_starts=seg_starts, pool_index=pool_index, gate_levels=gate_levels, gate_scale=gate_scale, up_levels=up_levels, up_scale=up_scale, down_levels=down_levels, down_scale=down_scale, shrink_weight=shrink_weight, expand_matrix_rows=expand_matrix_rows)


def dequantize(levels, scales):
    values = levels.astype(jnp.float32)
    rows = values.shape[0]
    groups = scales.shape[0]
    scaled = values.reshape(groups, rows // groups, values.shape[1]) * scales[:, None, :]
    return scaled.reshape(rows, values.shape[1]).astype(jnp.bfloat16)


def segment_tables(all_ids, seg_starts, pool_index, rows_dev):
    replicas = seg_starts.shape[0]
    positions = jnp.arange(rows_dev, dtype=jnp.int32)
    row_slot = jnp.sum((seg_starts[:, None, 1:] <= positions[None, :, None]).astype(jnp.int32), axis=2).astype(jnp.int32)
    clipped = jnp.minimum(seg_starts, rows_dev - 1)
    flat_rows = clipped + (jnp.arange(replicas, dtype=jnp.int32) * rows_dev)[:, None]
    slot_adapter = jnp.take(all_ids, flat_rows)
    slot_pool = jnp.take(pool_index, slot_adapter).astype(jnp.int32)
    following = jnp.concatenate([seg_starts[:, 1:], jnp.full((replicas, 1), rows_dev, jnp.int32)], axis=1)
    live = following > seg_starts
    row_pool = jnp.take_along_axis(slot_pool, row_slot, axis=1).astype(jnp.int32)
    return row_slot, slot_pool, live, row_pool


def reference(act_codes, act_scale, adapter_ids, seg_starts, pool_index, gate_levels, gate_scale, up_levels, up_scale, down_levels, down_scale, shrink_weight, expand_matrix_rows):
    inputs = act_codes
    row_slot, slot_pool, live, row_pool = segment_tables(adapter_ids, seg_starts, pool_index, ROWS_DEV)
    flat_pool = row_pool.reshape(-1)
    block = min(FF, 4096)
    count_blocks = FF // block

    def advance(carry, index):
        base_output, project = carry
        start = index * block
        w_gate = dequantize(lax.dynamic_slice_in_dim(gate_levels, start, block, 1), lax.dynamic_slice_in_dim(gate_scale, start, block, 1))
        w_up = dequantize(lax.dynamic_slice_in_dim(up_levels, start, block, 1), lax.dynamic_slice_in_dim(up_scale, start, block, 1))
        w_down = dequantize(lax.dynamic_slice_in_dim(down_levels, start, block, 0), lax.dynamic_slice_in_dim(down_scale, start // GROUP, block // GROUP, 0))
        shrink_rows = lax.dynamic_slice_in_dim(shrink_weight, start, block, 0)
        gate = act_scale[:, None] * jnp.dot(inputs, w_gate, preferred_element_type=jnp.float32)
        up = act_scale[:, None] * jnp.dot(inputs, w_up, preferred_element_type=jnp.float32)
        hidden = (jax.nn.silu(gate) * up).astype(jnp.bfloat16)
        base_output = base_output + jnp.dot(hidden, w_down, preferred_element_type=jnp.float32)
        project = project + jnp.dot(hidden, shrink_rows, preferred_element_type=jnp.float32)
        return (base_output, project), None

    start_carry = (jnp.zeros((ROWS_ALL, MODEL_WIDTH), jnp.float32), jnp.zeros((ROWS_ALL, ADAPTER_COUNT * ADAPTER_RANK), jnp.float32))
    (base_output, project), unused = lax.scan(advance, start_carry, jnp.arange(count_blocks, dtype=jnp.int32))
    choose = (flat_pool[:, None] == jnp.arange(ADAPTER_COUNT, dtype=jnp.int32)[None, :]).astype(jnp.float32)
    low = jnp.sum(project.reshape(ROWS_ALL, ADAPTER_COUNT, ADAPTER_RANK) * choose[:, :, None], axis=1).astype(jnp.bfloat16)
    spread_output = (choose[:, :, None] * low[:, None, :].astype(jnp.float32)).reshape(ROWS_ALL, ADAPTER_COUNT * ADAPTER_RANK).astype(jnp.bfloat16)
    adapter_delta = jnp.dot(spread_output, expand_matrix_rows.reshape(ADAPTER_COUNT * ADAPTER_RANK, MODEL_WIDTH), preferred_element_type=jnp.float32)
    return (base_output + adapter_delta).astype(jnp.bfloat16)
```

```python
import functools
import jax
import jax.numpy as jnp
from jax import lax
from jax.experimental import pallas as pl
from jax.experimental.pallas import tpu as pltpu
from jax.sharding import PartitionSpec as P

GROUP = 128
LANES = 128
MIB = 1024 * 1024


def vmem():
    return pl.BlockSpec(memory_space=pltpu.VMEM)


def smem():
    return pl.BlockSpec(memory_space=pltpu.SMEM)


def hbm():
    return pl.BlockSpec(memory_space=pltpu.HBM)


def scaled(levels, scales, first_group, groups):
    parts = []
    for g in range(groups):
        row = scales[pl.ds(first_group + g, 1), :].astype(jnp.bfloat16)
        parts.append(levels[g * GROUP : (g + 1) * GROUP, :] * row)
    return jnp.concatenate(parts, axis=0) if groups > 1 else parts[0]


def gate_up_kernel(pieces, blocks, first, last, kb, slots, offsets, *refs):
    rows_in = refs[: pieces * blocks]
    refs = refs[pieces * blocks :]
    gl, gs, ul, us = refs[:4]
    refs = refs[4:]
    if not first:
        gate_in, up_in = refs[:2]
        refs = refs[2:]
    if last:
        act_scale, hidden = refs[:2]
        refs = refs[2:]
        gate, up = refs[:2]
        refs = refs[2:]
    else:
        gate, up = refs[:2]
        refs = refs[2:]
    xs, gbuf, ubuf, sems = refs
    rows = rows_in[0].shape[0]
    depth = rows_in[0].shape[1]
    per_block = depth // kb
    steps = blocks * per_block

    def copies(step, slot):
        k = pl.multiple_of(offsets[step // per_block] + (step % per_block) * kb, kb)
        return (
            pltpu.make_async_copy(gl.at[pl.ds(k, kb), :], gbuf.at[slot], sems.at[0, slot]),
            pltpu.make_async_copy(ul.at[pl.ds(k, kb), :], ubuf.at[slot], sems.at[1, slot]),
        )

    for s in range(min(slots, steps)):
        for c in copies(s, s):
            c.start()
    for b in range(blocks):
        for p in range(pieces):
            for k in range(per_block):
                xs[b * per_block + k, p * rows : (p + 1) * rows, :] = rows_in[b * pieces + p][
                    :, k * kb : (k + 1) * kb
                ]
    if first:
        gate[...] = jnp.zeros_like(gate)
        up[...] = jnp.zeros_like(up)
    else:
        gate[...] = gate_in[...]
        up[...] = up_in[...]

    def body(step, carry):
        slot = lax.rem(step, slots)
        group = (offsets[step // per_block] + (step % per_block) * kb) // GROUP
        cg, cu = copies(step, slot)
        x = xs[step]
        cg.wait()
        gate[...] += jnp.dot(
            x, scaled(gbuf.at[slot], gs, group, kb // GROUP), preferred_element_type=jnp.float32
        )
        cu.wait()
        up[...] += jnp.dot(
            x, scaled(ubuf.at[slot], us, group, kb // GROUP), preferred_element_type=jnp.float32
        )

        @pl.when(step + slots < steps)
        def _():
            for c in copies(step + slots, slot):
                c.start()

        return carry

    lax.fori_loop(0, steps, body, 0)
    if last:
        g = gate[...] * act_scale[...]
        u = up[...] * act_scale[...]
        hidden[...] = (g / (1.0 + jnp.exp(-g)) * u).astype(jnp.bfloat16)


def gate_up(offsets, blocks_in, gl, gs, ul, us, acc, act_scale):
    first, last = acc is None, act_scale is not None
    blocks, pieces = len(blocks_in), len(blocks_in[0])
    rows, depth = blocks_in[0][0].shape
    width = gl.shape[1]
    kb = min(256, depth)
    slots = 6
    ins = [offsets] + [p for b in blocks_in for p in b] + [gl, gs, ul, us]
    specs = [smem()] + [vmem()] * (blocks * pieces) + [hbm(), vmem(), hbm(), vmem()]
    if not first:
        ins += list(acc)
        specs += [vmem(), vmem()]
    total = jax.ShapeDtypeStruct((rows * pieces, width), jnp.float32)
    scratch = []
    if last:
        ins.append(act_scale)
        specs.append(vmem())
        out_shape = [jax.ShapeDtypeStruct((rows * pieces, width), jnp.bfloat16)]
        scratch += [pltpu.VMEM(total.shape, jnp.float32)] * 2
    else:
        out_shape = [total, total]
    steps = blocks * depth // kb
    scratch += [
        pltpu.VMEM((steps, rows * pieces, kb), jnp.bfloat16),
        pltpu.VMEM((slots, kb, width), jnp.bfloat16),
        pltpu.VMEM((slots, kb, width), jnp.bfloat16),
        pltpu.SemaphoreType.DMA((2, slots)),
    ]
    return pl.pallas_call(
        functools.partial(gate_up_kernel, pieces, blocks, first, last, kb, slots),
        out_shape=out_shape,
        in_specs=specs,
        out_specs=[vmem()] * len(out_shape),
        scratch_shapes=scratch,
        compiler_params=pltpu.CompilerParams(vmem_limit_bytes=40 * MIB),
        cost_estimate=pl.CostEstimate(
            flops=4 * rows * pieces * blocks * depth * width,
            bytes_accessed=4 * blocks * depth * width,
            transcendentals=0,
        ),
        name="gate_up",
    )(*ins)


def down_kernel(kb, slots, shrink_too, offset, hidden, dl, ds, *refs):
    if shrink_too:
        shrink = refs[0]
        refs = refs[1:]
    mine, theirs, acc, scales, hs, buf, sems, scale_sem = refs
    depth, width = hidden.shape[1], acc.shape[1]
    half = mine.shape[0]
    steps = depth // kb
    col = pl.multiple_of(offset[0], width)

    def copy(step, slot):
        return pltpu.make_async_copy(
            dl.at[pl.ds(pl.multiple_of(step * kb, kb), kb), pl.ds(col, width)],
            buf.at[slot],
            sems.at[slot],
        )

    scale_copy = pltpu.make_async_copy(ds.at[:, pl.ds(col, width)], scales, scale_sem)
    scale_copy.start()
    for s in range(min(slots, steps)):
        copy(s, s).start()
    for s in range(steps):
        hs[s, :, :] = hidden[:, s * kb : (s + 1) * kb]
    acc[...] = jnp.zeros_like(acc)
    if shrink_too:
        project = jnp.dot(hidden[...], shrink[...], preferred_element_type=jnp.float32)
        project = project.astype(jnp.bfloat16)
        mine[:, width:] = project[:half]
        theirs[:, width:] = project[half:]
    scale_copy.wait()

    def body(step, carry):
        slot = lax.rem(step, slots)
        copy(step, slot).wait()
        acc[...] += jnp.dot(
            hs[step],
            scaled(buf.at[slot], scales, step * (kb // GROUP), kb // GROUP),
            preferred_element_type=jnp.float32,
        )

        @pl.when(step + slots < steps)
        def _():
            copy(step + slots, slot).start()

        return carry

    lax.fori_loop(0, steps, body, 0)
    mine[:, :width] = acc[:half, :].astype(jnp.bfloat16)
    theirs[:, :width] = acc[half:, :].astype(jnp.bfloat16)


def down(offset, hidden, dl, ds, width, shrink):
    rows, depth = hidden.shape
    kb = min(256, depth)
    slots = min(8, depth // kb)
    wide = width + (0 if shrink is None else shrink.shape[1])
    ins = [offset, hidden, dl, ds]
    specs = [smem(), vmem(), hbm(), hbm()]
    if shrink is not None:
        ins.append(shrink)
        specs.append(vmem())
    half = jax.ShapeDtypeStruct((rows // 2, wide), jnp.bfloat16)
    return pl.pallas_call(
        functools.partial(down_kernel, kb, slots, shrink is not None),
        out_shape=[half, half],
        in_specs=specs,
        out_specs=[vmem(), vmem()],
        scratch_shapes=[
            pltpu.VMEM((rows, width), jnp.float32),
            pltpu.VMEM((depth // GROUP, width), jnp.float32),
            pltpu.VMEM((depth // kb, rows, kb), jnp.bfloat16),
            pltpu.VMEM((slots, kb, width), jnp.bfloat16),
            pltpu.SemaphoreType.DMA((slots,)),
            pltpu.SemaphoreType.DMA,
        ],
        compiler_params=pltpu.CompilerParams(vmem_limit_bytes=24 * MIB),
        cost_estimate=pl.CostEstimate(
            flops=2 * rows * depth * width, bytes_accessed=2 * depth * width, transcendentals=0
        ),
        name="down",
    )(*ins)


def fold_matrix(pool_width, rank, lanes, transposed):
    shape = (lanes, pool_width) if transposed else (pool_width, lanes)
    wide = lax.broadcasted_iota(jnp.int32, shape, 1 if transposed else 0)
    slim = lax.broadcasted_iota(jnp.int32, shape, 0 if transposed else 1)
    return (lax.rem(wide, rank) == slim).astype(jnp.float32).astype(jnp.bfloat16)


def pool_mask(pool_row, rows, pool_width, rank):
    column = lax.broadcasted_iota(jnp.int32, (rows, pool_width), 1)
    start = pool_row[...] * rank
    return (column >= start) & (column < start + rank)


def message_kernel(count, width, rank, pool_row, *refs):
    parts, (out, low) = refs[:count], refs[count:]
    total = parts[0][...].astype(jnp.float32)
    for p in parts[1:]:
        total = total + p[...].astype(jnp.float32)
    rows, wide = total.shape
    mask = pool_mask(pool_row, rows, wide - width, rank)
    chosen = jnp.where(mask, total[:, width:], 0.0).astype(jnp.bfloat16)
    part = jnp.dot(
        chosen,
        fold_matrix(wide - width, rank, low.shape[1], False),
        preferred_element_type=jnp.float32,
    ).astype(jnp.bfloat16)
    low[...] = part
    out[:, :width] = total[:, :width].astype(jnp.bfloat16)
    out[:, width:] = part


def message(parts, pool_row, width, rank):
    rows = parts[0].shape[0]
    lanes = max(LANES, rank)
    return pl.pallas_call(
        functools.partial(message_kernel, len(parts), width, rank),
        out_shape=[
            jax.ShapeDtypeStruct((rows, width + lanes), jnp.bfloat16),
            jax.ShapeDtypeStruct((rows, lanes), jnp.bfloat16),
        ],
        in_specs=[vmem()] * (1 + len(parts)),
        out_specs=[vmem()] * 2,
        name="message",
    )(pool_row, *parts)


def final_kernel(count, wides, rank, pool_row, low, pool, *refs):
    parts, wide, out = refs[:count], refs[count : count + wides], refs[count + wides]
    rows, width = out.shape
    total_low = low[...].astype(jnp.float32)
    for w in wide:
        total_low = total_low + w[:, width:].astype(jnp.float32)
    total_low = total_low.astype(jnp.bfloat16)
    pool_width = pool.shape[0]
    spread = jnp.dot(
        total_low,
        fold_matrix(pool_width, rank, total_low.shape[1], True),
        preferred_element_type=jnp.float32,
    )
    mask = pool_mask(pool_row, rows, pool_width, rank)
    spread = jnp.where(mask, spread, 0.0).astype(jnp.bfloat16)
    total = jnp.dot(spread, pool[...], preferred_element_type=jnp.float32)
    for p in parts:
        total = total + p[...].astype(jnp.float32)
    for w in wide:
        total = total + w[:, :width].astype(jnp.float32)
    out[...] = total.astype(jnp.bfloat16)


def final(parts, wide, pool_row, low, pool, rank):
    rows, width = parts[0].shape
    return pl.pallas_call(
        functools.partial(final_kernel, len(parts), len(wide), rank),
        out_shape=jax.ShapeDtypeStruct((rows, width), jnp.bfloat16),
        in_specs=[vmem()] * (3 + len(parts) + len(wide)),
        out_specs=vmem(),
        compiler_params=pltpu.CompilerParams(vmem_limit_bytes=16 * MIB),
        name="final",
    )(pool_row, low, pool, *parts, *wide)


def add_bf16(a, b):
    return (a.astype(jnp.float32) + b.astype(jnp.float32)).astype(jnp.bfloat16)


def nearest_first(count):
    return sorted(range(1, count), key=lambda d: (d.bit_length(), -d))


def local(replicas, tensors, *args):
    (
        act_codes,
        act_scale,
        adapter_ids,
        seg_starts,
        pool_index,
        gate_levels,
        gate_scale,
        up_levels,
        up_scale,
        down_levels,
        down_scale,
        shrink_weight,
        expand_rows,
    ) = args
    replica = lax.axis_index("replica")
    tensor = lax.axis_index("tensor")
    cores = 2
    chips = replicas // cores
    rows, depth = act_codes.shape
    rank, width = expand_rows.shape[1], expand_rows.shape[2]

    def core_swap(v):
        return lax.ppermute(v, "replica", [(r, r ^ 1) for r in range(replicas)])

    def chip_swap(v, s):
        return lax.ppermute(v, "replica", [(r, r ^ (s * cores)) for r in range(replicas)])

    def tensor_swap(v, d):
        return lax.ppermute(v, "tensor", [(t, t ^ d) for t in range(tensors)])

    order = [s * cores for s in range(chips)] + [s * cores + 1 for s in range(chips)]

    def spread_block(v):
        same = [v] + [chip_swap(v, s) for s in range(1, chips)]
        return same + [core_swap(p) for p in same]

    distances = [0] + nearest_first(tensors)
    offsets = jnp.stack([(tensor ^ d) for d in distances]).astype(jnp.int32)
    row_scale = jnp.concatenate(
        [
            lax.dynamic_slice_in_dim(act_scale, (replica ^ o) * rows, rows, 0)
            for o in order
        ]
    )[:, None]
    own_choice = adapter_ids[:, None] == jnp.arange(pool_index.shape[0], dtype=jnp.int32)[None, :]
    pool_row = jnp.sum(jnp.where(own_choice, pool_index[None, :], 0), axis=1, keepdims=True)
    whole_pool = lax.all_gather(expand_rows, "replica", axis=0, tiled=True)
    whole_pool = whole_pool.reshape(-1, width)

    arrived = {0: spread_block(act_codes)}
    moved = {d: tensor_swap(act_codes, d) for d in distances[1:]}
    for d in distances[1:]:
        arrived[d] = spread_block(moved[d])
    groups = [distances[:1]]
    rest = distances[1:]
    if len(rest) <= 3:
        groups += [[d] for d in rest]
    else:
        groups += [rest[: len(rest) // 2], rest[len(rest) // 2 :]]
    acc = None
    at = 0
    for i, g in enumerate(groups):
        acc = gate_up(
            offsets[at : at + len(g)] * depth,
            [arrived[d] for d in g],
            gate_levels,
            gate_scale,
            up_levels,
            up_scale,
            acc,
            row_scale if i == len(groups) - 1 else None,
        )
        at += len(g)
    hidden = acc[0]

    low = None
    received = []
    for d in distances[1:][::-1] + [0]:
        i = distances.index(d)
        first = low is None
        mine, theirs = down(
            offsets[i : i + 1] * width,
            hidden,
            down_levels,
            down_scale,
            width,
            shrink_weight if first else None,
        )
        pair = add_bf16(mine, core_swap(theirs))
        parts = [pair[:rows]] + [
            chip_swap(pair[s * rows : (s + 1) * rows], s) for s in range(1, chips)
        ]
        if first:
            out, low = message(parts, pool_row, width, rank)
            received.append(tensor_swap(out, d))
        elif d:
            total = parts[0].astype(jnp.float32)
            for p in parts[1:]:
                total = total + p.astype(jnp.float32)
            out = jnp.concatenate([total.astype(jnp.bfloat16), low], axis=1)
            received.append(tensor_swap(out, d))
        else:
            own = parts
    return final(own, received, pool_row, low, whole_pool, rank)


def solution(mesh):
    placed = (
        P(("parts", "replica"), "tensor"),
        P("parts"),
        P(("parts", "replica")),
        P("parts", None),
        P("parts"),
        P(None, ("replica", "tensor")),
        P(None, ("replica", "tensor")),
        P(None, ("replica", "tensor")),
        P(None, ("replica", "tensor")),
        P(("replica", "tensor"), None),
        P(("replica", "tensor"), None),
        P(("replica", "tensor"), None),
        P("replica", None, "tensor"),
    )
    return jax.shard_map(
        functools.partial(local, mesh.shape["replica"], mesh.shape["tensor"]),
        mesh=mesh,
        in_specs=placed,
        out_specs=P(("parts", "replica"), "tensor"),
        check_vma=False,
    )
```

```python
import functools
import jax
import jax.numpy as jnp
from jax import lax
from jax.experimental import pallas as pl
from jax.experimental.pallas import tpu as pltpu
from jax.sharding import PartitionSpec as P

GROUP = 128
LANES = 128
MIB = 1024 * 1024
BLOCK = 512


def vmem():
    return pl.BlockSpec(memory_space=pltpu.VMEM)


def smem():
    return pl.BlockSpec(memory_space=pltpu.SMEM)


def hbm():
    return pl.BlockSpec(memory_space=pltpu.HBM)


def anywhere():
    return pl.BlockSpec(memory_space=pl.ANY)


def after(value, *earlier):
    return lax.optimization_barrier((value,) + earlier)[0]


def scaled(levels, scales, first_group, groups):
    parts = []
    for g in range(groups):
        row = scales[pl.ds(first_group + g, 1), :].astype(jnp.bfloat16)
        parts.append(levels[g * GROUP : (g + 1) * GROUP, :] * row)
    return jnp.concatenate(parts, axis=0) if groups > 1 else parts[0]


def as_column(row):
    rows = row.shape[1]
    place = lax.broadcasted_iota(jnp.int32, (rows, rows), 0)
    same = place == lax.broadcasted_iota(jnp.int32, (rows, rows), 1)
    return jnp.sum(jnp.where(same, row, jnp.zeros_like(row)), axis=1, keepdims=True)


def fill_kernel(
    kb, count, depth, order, where, pool_index, act_scale, ids,
    gl, gs, ul, us, ds, gbuf, ubuf, gs_out, us_out, ds_out, row_scale, pool_row,
    pool_held, act_held, ids_held, act_column, small_sems, sems,
):
    k = pl.multiple_of(where[1] * depth, kb)
    small = [(pool_index, pool_held), (act_scale, act_held), (ids, ids_held)]
    small = [pltpu.make_async_copy(a, b, small_sems.at[i]) for i, (a, b) in enumerate(small)]
    for c in small:
        c.start()
    moves = [(gs, gs_out), (us, us_out), (ds, ds_out)]
    for j in range(count):
        rows = pl.ds(k + j * kb, kb)
        moves += [(gl.at[rows, :], gbuf.at[j]), (ul.at[rows, :], ubuf.at[j])]
    made = [pltpu.make_async_copy(a, b, sems.at[i]) for i, (a, b) in enumerate(moves)]
    for c in made:
        c.start()
    for c in small:
        c.wait()
    rows = ids.shape[1]
    act_column[...] = as_column(act_held[...])
    for p, o in enumerate(order):
        at = pl.multiple_of((where[0] ^ o) * rows, rows)
        row_scale[p * rows : (p + 1) * rows, :] = act_column[pl.ds(at, rows), :]
    column = as_column(ids_held[...].astype(jnp.float32)).astype(jnp.int32)
    named = lax.broadcasted_iota(jnp.int32, (rows, pool_held.shape[1]), 1) == column
    chosen = jnp.where(named, pool_held[...].astype(jnp.float32), 0.0)
    pool_row[...] = jnp.sum(chosen, axis=1, keepdims=True).astype(jnp.int32)
    for c in made:
        c.wait()


def fill(where, pool_index, act_scale, ids, order, depth, gl, gs, ul, us, ds, kb, count):
    block = pltpu.VMEM((count, kb, gl.shape[1]), gl.dtype)
    out_shape = [block, block] + [jax.ShapeDtypeStruct(v.shape, v.dtype) for v in (gs, us, ds)]
    rows = ids.shape[1]
    out_shape += [
        jax.ShapeDtypeStruct((rows * len(order), 1), jnp.float32),
        jax.ShapeDtypeStruct((rows, 1), jnp.int32),
    ]
    return pl.pallas_call(
        functools.partial(fill_kernel, kb, count, depth, order),
        out_shape=out_shape,
        in_specs=[smem()] + [anywhere()] * 3 + [hbm()] * 5,
        out_specs=[vmem()] * 7,
        scratch_shapes=[
            pltpu.VMEM(pool_index.shape, jnp.int32),
            pltpu.VMEM(act_scale.shape, jnp.float32),
            pltpu.VMEM(ids.shape, jnp.int32),
            pltpu.VMEM((act_scale.shape[1], 1), jnp.float32),
            pltpu.SemaphoreType.DMA((3,)),
            pltpu.SemaphoreType.DMA((3 + 2 * count,)),
        ],
        compiler_params=pltpu.CompilerParams(vmem_limit_bytes=4 * MIB),
        cost_estimate=pl.CostEstimate(
            flops=0, bytes_accessed=4 * count * kb * gl.shape[1], transcendentals=0
        ),
        name="fill",
    )(where, pool_index, act_scale, ids, gl, gs, ul, us, ds)


def run(steps, stage, ahead):
    for c in ahead:
        c.start()

    def body(step, carry):
        stage(step)
        return carry

    lax.fori_loop(0, steps, body, 0)
    for c in ahead:
        c.wait()


def gate_up_kernel(pieces, distances, coming, first, last, kb, ahead, where, *refs):
    blocks = len(distances)
    rows_in = refs[: pieces * blocks]
    refs = refs[pieces * blocks :]
    gl, gs, ul, us, g_held, u_held = refs[:6]
    refs = refs[6:]
    if not first:
        gate_in, up_in = refs[:2]
        refs = refs[2:]
    if last:
        act_scale, dl, hidden, d_next = refs[:4]
        refs = refs[4:]
        gate, up = refs[:2]
        refs = refs[2:]
    else:
        gate, up, g_next, u_next = refs[:4]
        refs = refs[4:]
    xs, row_sems, ahead_sems = refs
    rows = rows_in[0].shape[0]
    depth = rows_in[0].shape[1]
    per_block = depth // kb
    steps = blocks * per_block

    row_copies = [
        pltpu.make_async_copy(
            rows_in[b * pieces + p],
            xs.at[p * rows : (p + 1) * rows, b * depth : (b + 1) * depth],
            row_sems.at[b * pieces + p],
        )
        for b in range(blocks)
        for p in range(pieces)
    ]
    for c in row_copies:
        c.start()

    def place(step):
        block = where[1] ^ distances[0]
        for b in range(1, blocks):
            block = jnp.where(step // per_block == b, where[1] ^ distances[b], block)
        return pl.multiple_of(block * depth + (step % per_block) * kb, kb)

    following = []
    for j in range(ahead):
        if last:
            down_kb, width = d_next.shape[1:]
            col = pl.multiple_of((where[1] ^ coming[0]) * width, width)
            source = dl.at[j * down_kb : (j + 1) * down_kb, pl.ds(col, width)]
            following.append(pltpu.make_async_copy(source, d_next.at[j], ahead_sems.at[j]))
        else:
            k = (where[1] ^ coming[j // per_block]) * depth + (j % per_block) * kb
            k = pl.multiple_of(k, kb)
            for i, (a, b) in enumerate(((gl, g_next), (ul, u_next))):
                following.append(
                    pltpu.make_async_copy(
                        a.at[pl.ds(k, kb), :], b.at[j], ahead_sems.at[2 * j + i]
                    )
                )

    def add(total, given, scales, step):
        block = given.at[step]
        group = place(step) // GROUP
        total[...] += jnp.dot(
            xs[:, pl.ds(pl.multiple_of(step * kb, kb), kb)],
            scaled(block, scales, group, kb // GROUP),
            preferred_element_type=jnp.float32,
        )

    if first:
        gate[...] = jnp.zeros_like(gate)
        up[...] = jnp.zeros_like(up)
    else:
        gate[...] = gate_in[...]
        up[...] = up_in[...]
    for c in row_copies:
        c.wait()
    def both(step):
        add(gate, g_held, gs, step)
        add(up, u_held, us, step)

    run(steps, both, following)
    if last:
        g = gate[...] * act_scale[...]
        u = up[...] * act_scale[...]
        hidden[...] = (g / (1.0 + jnp.exp(-g)) * u).astype(jnp.bfloat16)


def gate_up(where, distances, coming, blocks_in, gl, gs, ul, us, carried, acc, act_scale, dl, kb, down_kb, ahead):
    first, last = acc is None, act_scale is not None
    blocks, pieces = len(blocks_in), len(blocks_in[0])
    rows, depth = blocks_in[0][0].shape
    width = gl.shape[1]
    ins = [where] + [p for b in blocks_in for p in b] + [gl, gs, ul, us] + list(carried)
    specs = [smem()] + [anywhere()] * (blocks * pieces) + [hbm(), vmem(), hbm(), vmem()]
    specs += [vmem(), vmem()]
    if not first:
        ins += list(acc)
        specs += [vmem(), vmem()]
    total = jax.ShapeDtypeStruct((rows * pieces, width), jnp.float32)
    scratch = []
    if last:
        ins += [act_scale, dl]
        specs += [vmem(), hbm()]
        out_shape = [jax.ShapeDtypeStruct((rows * pieces, width), jnp.bfloat16)]
        out_shape += [pltpu.VMEM((ahead, down_kb, depth), jnp.bfloat16)]
        scratch += [pltpu.VMEM(total.shape, jnp.float32)] * 2
    else:
        out_shape = [total, total] + [pltpu.VMEM((ahead, kb, width), jnp.bfloat16)] * 2
    scratch += [
        pltpu.VMEM((rows * pieces, blocks * depth), jnp.bfloat16),
        pltpu.SemaphoreType.DMA((blocks * pieces,)),
        pltpu.SemaphoreType.DMA((2 * ahead,)),
    ]
    return pl.pallas_call(
        functools.partial(gate_up_kernel, pieces, distances, coming, first, last, kb, ahead),
        out_shape=out_shape,
        in_specs=specs,
        out_specs=[vmem()] * len(out_shape),
        scratch_shapes=scratch,
        compiler_params=pltpu.CompilerParams(vmem_limit_bytes=8 * MIB),
        cost_estimate=pl.CostEstimate(
            flops=4 * rows * pieces * blocks * depth * width,
            bytes_accessed=4 * blocks * depth * width,
            transcendentals=0,
        ),
        name="gate_up",
    )(*ins)


def down_kernel(distances, kb, ahead, shrink_too, where, hidden, dl, ds, d_held, *refs):
    if shrink_too:
        shrink = refs[0]
        refs = refs[1:]
    mine, theirs = refs[:2]
    refs = refs[2:]
    if ahead:
        d_next = refs[0]
        refs = refs[1:]
    acc, ahead_sems = refs
    depth, width = hidden.shape[1], acc.shape[1]
    half = mine.shape[0]
    steps = depth // kb
    col = pl.multiple_of((where[1] ^ distances[0]) * width, width)

    following = []
    for j in range(ahead):
        next_col = pl.multiple_of((where[1] ^ distances[1]) * width, width)
        source = dl.at[j * kb : (j + 1) * kb, pl.ds(next_col, width)]
        following.append(pltpu.make_async_copy(source, d_next.at[j], ahead_sems.at[j]))

    def add(step):
        block = d_held.at[step]
        parts = []
        for g in range(kb // GROUP):
            row = ds[pl.ds(step * (kb // GROUP) + g, 1), pl.ds(col, width)].astype(jnp.bfloat16)
            parts.append(block[g * GROUP : (g + 1) * GROUP, :] * row)
        weight = jnp.concatenate(parts, axis=0) if len(parts) > 1 else parts[0]
        acc[...] += jnp.dot(
            hidden[:, pl.ds(pl.multiple_of(step * kb, kb), kb)],
            weight,
            preferred_element_type=jnp.float32,
        )

    def project():
        low = jnp.dot(hidden[...], shrink[...], preferred_element_type=jnp.float32)
        mine[:, width:] = low[:half]
        theirs[:, width:] = low[half:].astype(jnp.bfloat16)

    acc[...] = jnp.zeros_like(acc)
    run(steps, add, following)
    if shrink_too:
        project()
    mine[:, :width] = acc[:half, :]
    theirs[:, :width] = acc[half:, :].astype(jnp.bfloat16)


def down(where, distances, hidden, dl, ds, carried, width, shrink, kb, ahead):
    rows, depth = hidden.shape
    wide = width + (0 if shrink is None else shrink.shape[1])
    ins = [where, hidden, dl, ds, carried]
    specs = [smem(), vmem(), hbm(), vmem(), vmem()]
    if shrink is not None:
        ins.append(shrink)
        specs.append(vmem())
    out_shape = [
        jax.ShapeDtypeStruct((rows // 2, wide), jnp.float32),
        jax.ShapeDtypeStruct((rows // 2, wide), jnp.bfloat16),
    ]
    if ahead:
        out_shape.append(pltpu.VMEM((ahead, kb, width), jnp.bfloat16))
    return pl.pallas_call(
        functools.partial(down_kernel, distances, kb, ahead, shrink is not None),
        out_shape=out_shape,
        in_specs=specs,
        out_specs=[vmem()] * len(out_shape),
        scratch_shapes=[
            pltpu.VMEM((rows, width), jnp.float32),
            pltpu.SemaphoreType.DMA((max(1, ahead),)),
        ],
        compiler_params=pltpu.CompilerParams(vmem_limit_bytes=8 * MIB),
        cost_estimate=pl.CostEstimate(
            flops=2 * rows * depth * width, bytes_accessed=2 * depth * width, transcendentals=0
        ),
        name="down",
    )(*ins)


def cost(count):
    return pl.CostEstimate(flops=count, bytes_accessed=4 * count, transcendentals=0)


def pair_kernel(chips, mine, got, own, *send):
    rows = own.shape[0]
    own[...] = mine[:rows, :] + got[:rows, :].astype(jnp.float32)
    for s in range(1, chips):
        at = slice(s * rows, (s + 1) * rows)
        send[s - 1][...] = (mine[at, :] + got[at, :].astype(jnp.float32)).astype(jnp.bfloat16)


def pair_sum(mine, got, chips):
    rows, width = mine.shape[0] // chips, mine.shape[1]
    out_shape = [jax.ShapeDtypeStruct((rows, width), jnp.float32)]
    out_shape += [jax.ShapeDtypeStruct((rows, width), jnp.bfloat16)] * (chips - 1)
    return pl.pallas_call(
        functools.partial(pair_kernel, chips),
        out_shape=out_shape,
        in_specs=[vmem()] * 2,
        out_specs=[vmem()] * chips,
        compiler_params=pltpu.CompilerParams(vmem_limit_bytes=4 * MIB),
        cost_estimate=cost(rows * chips * width),
        name="pair",
    )(mine, got)


def attach_kernel(count, low, *refs):
    parts, out = refs[:count], refs[count]
    width = parts[0].shape[1]
    total = parts[0][...]
    for p in parts[1:]:
        total = total + p[...].astype(jnp.float32)
    out[:, :width] = total.astype(jnp.bfloat16)
    out[:, width:] = low[...]


def attach(parts, low):
    rows, width = parts[0].shape
    return pl.pallas_call(
        functools.partial(attach_kernel, len(parts)),
        out_shape=jax.ShapeDtypeStruct((rows, width + low.shape[1]), jnp.bfloat16),
        in_specs=[vmem()] * (1 + len(parts)),
        out_specs=vmem(),
        compiler_params=pltpu.CompilerParams(vmem_limit_bytes=4 * MIB),
        cost_estimate=cost(rows * width * len(parts)),
        name="attach",
    )(low, *parts)


def fold_matrix(pool_width, rank, lanes, transposed):
    shape = (lanes, pool_width) if transposed else (pool_width, lanes)
    wide = lax.broadcasted_iota(jnp.int32, shape, 1 if transposed else 0)
    slim = lax.broadcasted_iota(jnp.int32, shape, 0 if transposed else 1)
    return (lax.rem(wide, rank) == slim).astype(jnp.float32).astype(jnp.bfloat16)


def pool_mask(pool_row, rows, pool_width, rank):
    column = lax.broadcasted_iota(jnp.int32, (rows, pool_width), 1)
    start = pool_row * rank
    return (column >= start) & (column < start + rank)


def message_kernel(count, width, rank, pool_row, *refs):
    parts, (out, low) = refs[:count], refs[count:]
    total = parts[0][...].astype(jnp.float32)
    for p in parts[1:]:
        total = total + p[...].astype(jnp.float32)
    rows, wide = total.shape
    mask = pool_mask(pool_row[...], rows, wide - width, rank)
    chosen = jnp.where(mask, total[:, width:], 0.0).astype(jnp.bfloat16)
    part = jnp.dot(
        chosen,
        fold_matrix(wide - width, rank, low.shape[1], False),
        preferred_element_type=jnp.float32,
    ).astype(jnp.bfloat16)
    low[...] = part
    out[:, :width] = total[:, :width].astype(jnp.bfloat16)
    out[:, width:] = part


def message(parts, pool_row, width, rank):
    rows = parts[0].shape[0]
    lanes = max(LANES, rank)
    return pl.pallas_call(
        functools.partial(message_kernel, len(parts), width, rank),
        out_shape=[
            jax.ShapeDtypeStruct((rows, width + lanes), jnp.bfloat16),
            jax.ShapeDtypeStruct((rows, lanes), jnp.bfloat16),
        ],
        in_specs=[vmem()] * (1 + len(parts)),
        out_specs=[vmem()] * 2,
        compiler_params=pltpu.CompilerParams(vmem_limit_bytes=6 * MIB),
        cost_estimate=cost(rows * width * len(parts)),
        name="message",
    )(pool_row, *parts)


def final_kernel(count, wides, order, rank, where, pool_row, low, *refs):
    pieces = len(order)
    pool, refs = refs[:pieces], refs[pieces:]
    parts, wide, out = refs[:count], refs[count : count + wides], refs[count + wides]
    rows, width = out.shape
    total_low = low[...].astype(jnp.float32)
    for w in wide:
        total_low = total_low + w[:, width:].astype(jnp.float32)
    total_low = total_low.astype(jnp.bfloat16)
    pool_width = pool[0].shape[0]
    spread = jnp.dot(
        total_low,
        fold_matrix(pool_width, rank, total_low.shape[1], True),
        preferred_element_type=jnp.float32,
    )
    total = jnp.zeros((rows, width), jnp.float32)
    for p in range(pieces):
        held = pool_row[...] - (where[0] ^ order[p]) * (pool_width // rank)
        mask = pool_mask(held, rows, pool_width, rank)
        chosen = jnp.where(mask, spread, 0.0).astype(jnp.bfloat16)
        total = total + jnp.dot(chosen, pool[p][...], preferred_element_type=jnp.float32)
    for p in parts:
        total = total + p[...].astype(jnp.float32)
    for w in wide:
        total = total + w[:, :width].astype(jnp.float32)
    out[...] = total.astype(jnp.bfloat16)


def final(parts, wide, where, order, pool_row, low, pool, rank):
    rows, width = parts[0].shape
    return pl.pallas_call(
        functools.partial(final_kernel, len(parts), len(wide), order, rank),
        out_shape=jax.ShapeDtypeStruct((rows, width), jnp.bfloat16),
        in_specs=[smem()] + [vmem()] * (2 + len(pool) + len(parts) + len(wide)),
        out_specs=vmem(),
        compiler_params=pltpu.CompilerParams(vmem_limit_bytes=4 * MIB),
        name="final",
            cost_estimate=cost(0),
    )(where, pool_row, low, *pool, *parts, *wide)


def nearest_first(count):
    return sorted(range(1, count), key=lambda d: (d.bit_length(), -d))


def local(replicas, tensors, *args):
    (
        act_codes,
        act_scale,
        adapter_ids,
        seg_starts,
        pool_index,
        gate_levels,
        gate_scale,
        up_levels,
        up_scale,
        down_levels,
        down_scale,
        shrink_weight,
        expand_rows,
    ) = args
    replica = lax.axis_index("replica")
    tensor = lax.axis_index("tensor")
    cores = 2
    chips = replicas // cores
    rows, depth = act_codes.shape
    rank, width = expand_rows.shape[1], expand_rows.shape[2]
    hidden_rows = down_levels.shape[0]

    def core_swap(v):
        return lax.ppermute(v, "replica", [(r, r ^ 1) for r in range(replicas)])

    def chip_swap(v, s):
        return lax.ppermute(v, "replica", [(r, r ^ (s * cores)) for r in range(replicas)])

    def tensor_swap(v, d):
        return lax.ppermute(v, "tensor", [(t, t ^ d) for t in range(tensors)])

    order = [s * cores for s in range(chips)] + [s * cores + 1 for s in range(chips)]

    def spread_block(v):
        same = [v] + [chip_swap(v, s) for s in range(1, chips)]
        return same + [core_swap(p) for p in same]

    gate_levels, up_levels, down_levels, gate_scale, up_scale, down_scale = (
        pltpu.with_memory_space_constraint(v, pltpu.HBM)
        for v in (gate_levels, up_levels, down_levels, gate_scale, up_scale, down_scale)
    )
    near = [0] + nearest_first(tensors)
    far = near[1:][::-1] + [0]
    kb = min(BLOCK, depth)
    down_kb = min(BLOCK, hidden_rows)
    where = jnp.stack([replica, tensor]).astype(jnp.int32)

    groups = [near[:1]]
    rest = near[1:]
    if len(rest) <= 3:
        groups += [[d] for d in rest]
    else:
        groups += [rest[: len(rest) // 2], rest[len(rest) // 2 :]]

    moved = {d: tensor_swap(act_codes, d) for d in groups[1]}
    same = [act_codes] + [chip_swap(act_codes, s) for s in range(1, chips)]
    filled = fill(
        where,
        *(
            pltpu.with_memory_space_constraint(v[None, :], pltpu.HBM)
            for v in (pool_index, act_scale, adapter_ids)
        ),
        order,
        depth,
        gate_levels,
        gate_scale,
        up_levels,
        up_scale,
        down_scale,
        kb,
        depth // kb,
    )
    carried = filled[:2]
    gate_scale, up_scale, down_scale, row_scale, pool_row = filled[2:]
    arrived = {0: same + [core_swap(after(p, pool_row)) for p in same]}
    codes_later = after(act_codes, pool_row)
    for d in groups[1]:
        arrived[d] = spread_block(after(moved[d], pool_row))
    for late in groups[2:]:
        for d in late:
            moved[d] = tensor_swap(codes_later, d)
    acc = None
    for i, g in enumerate(groups):
        is_last = i == len(groups) - 1
        following = far[:1] if is_last else groups[i + 1]
        out = gate_up(
            where,
            g,
            following,
            [arrived[d] for d in g],
            gate_levels,
            gate_scale,
            up_levels,
            up_scale,
            carried,
            acc,
            row_scale if is_last else None,
            down_levels,
            kb,
            down_kb,
            hidden_rows // down_kb if is_last else len(following) * depth // kb,
        )
        if is_last:
            hidden, carried = out
        else:
            acc, carried = out[:2], out[2:]
        if i == 0:
            for late in groups[2:]:
                for d in late:
                    arrived[d] = spread_block(after(moved[d], acc[0]))
        if i == 1:
            pool = spread_block(after(expand_rows.reshape(-1, width), acc[0]))

    low = None
    received = []
    sent, sums, messages = [], [], []
    for n, d in enumerate(far):
        more = n + 1 < len(far)
        source = hidden
        if n >= 2:
            source = after(source, sums[n - 2])
        if n >= 3:
            source = after(source, messages[n - 3])
        out = down(
            where,
            [d] + far[n + 1 : n + 2],
            source,
            down_levels,
            down_scale,
            carried,
            width,
            shrink_weight if n == 0 else None,
            down_kb,
            hidden_rows // down_kb if more else 0,
        )
        mine, theirs = out[:2]
        carried = out[2] if more else None
        own, *send = pair_sum(mine, core_swap(theirs), chips)
        sums.append(send[0])
        parts = [own] + [chip_swap(send[s - 1], s) for s in range(1, chips)]
        if n == 0:
            block, low = message(parts, pool_row, width, rank)
        elif d:
            block = attach(parts, low)
        if d:
            messages.append(block)
            received.append(tensor_swap(block, d))
    return final(parts, received, where, order, pool_row, low, pool, rank)


def solution(mesh):
    placed = (
        P(("parts", "replica"), "tensor"),
        P("parts"),
        P(("parts", "replica")),
        P("parts", None),
        P("parts"),
        P(None, ("replica", "tensor")),
        P(None, ("replica", "tensor")),
        P(None, ("replica", "tensor")),
        P(None, ("replica", "tensor")),
        P(("replica", "tensor"), None),
        P(("replica", "tensor"), None),
        P(("replica", "tensor"), None),
        P("replica", None, "tensor"),
    )
    return jax.shard_map(
        functools.partial(local, mesh.shape["replica"], mesh.shape["tensor"]),
        mesh=mesh,
        in_specs=placed,
        out_specs=P(("parts", "replica"), "tensor"),
        check_vma=False,
    )
```

```python
import functools
import jax
import jax.numpy as jnp
from jax import lax
from jax.experimental import pallas as pl
from jax.experimental.pallas import tpu as pltpu
from jax.sharding import PartitionSpec as P

GROUP = 128
LANES = 128
MIB = 1024 * 1024
BLOCK = 512


def vmem():
    return pl.BlockSpec(memory_space=pltpu.VMEM)


def smem():
    return pl.BlockSpec(memory_space=pltpu.SMEM)


def hbm():
    return pl.BlockSpec(memory_space=pltpu.HBM)


def anywhere():
    return pl.BlockSpec(memory_space=pl.ANY)


def after(value, *earlier):
    return lax.optimization_barrier((value,) + earlier)[0]


def scaled(levels, scales, first_group, groups):
    parts = []
    for g in range(groups):
        row = scales[pl.ds(first_group + g, 1), :].astype(jnp.bfloat16)
        parts.append(levels[g * GROUP : (g + 1) * GROUP, :] * row)
    return jnp.concatenate(parts, axis=0) if groups > 1 else parts[0]


def as_column(row):
    rows = row.shape[1]
    place = lax.broadcasted_iota(jnp.int32, (rows, rows), 0)
    same = place == lax.broadcasted_iota(jnp.int32, (rows, rows), 1)
    return jnp.sum(jnp.where(same, row, jnp.zeros_like(row)), axis=1, keepdims=True)


def fill_kernel(
    kb, count, depth, order, where, pool_index, act_scale, ids,
    gl, gs, ul, us, ds, gbuf, ubuf, gs_out, us_out, ds_out, row_scale, pool_row,
    pool_held, act_held, ids_held, act_column, small_sems, sems,
):
    k = pl.multiple_of(where[1] * depth, kb)
    small = [(pool_index, pool_held), (act_scale, act_held), (ids, ids_held)]
    small = [pltpu.make_async_copy(a, b, small_sems.at[i]) for i, (a, b) in enumerate(small)]
    for c in small:
        c.start()
    moves = [(gs, gs_out), (us, us_out), (ds, ds_out)]
    for j in range(count):
        rows = pl.ds(k + j * kb, kb)
        moves += [(gl.at[rows, :], gbuf.at[j]), (ul.at[rows, :], ubuf.at[j])]
    made = [pltpu.make_async_copy(a, b, sems.at[i]) for i, (a, b) in enumerate(moves)]
    for c in made:
        c.start()
    for c in small:
        c.wait()
    rows = ids.shape[1]
    act_column[...] = as_column(act_held[...])
    for p, o in enumerate(order):
        at = pl.multiple_of((where[0] ^ o) * rows, rows)
        row_scale[p * rows : (p + 1) * rows, :] = act_column[pl.ds(at, rows), :]
    column = as_column(ids_held[...].astype(jnp.float32)).astype(jnp.int32)
    named = lax.broadcasted_iota(jnp.int32, (rows, pool_held.shape[1]), 1) == column
    chosen = jnp.where(named, pool_held[...].astype(jnp.float32), 0.0)
    pool_row[...] = jnp.sum(chosen, axis=1, keepdims=True).astype(jnp.int32)
    for c in made:
        c.wait()


def fill(where, pool_index, act_scale, ids, order, depth, gl, gs, ul, us, ds, kb, count):
    block = pltpu.VMEM((count, kb, gl.shape[1]), gl.dtype)
    out_shape = [block, block] + [jax.ShapeDtypeStruct(v.shape, v.dtype) for v in (gs, us, ds)]
    rows = ids.shape[1]
    out_shape += [
        jax.ShapeDtypeStruct((rows * len(order), 1), jnp.float32),
        jax.ShapeDtypeStruct((rows, 1), jnp.int32),
    ]
    return pl.pallas_call(
        functools.partial(fill_kernel, kb, count, depth, order),
        out_shape=out_shape,
        in_specs=[smem()] + [anywhere()] * 3 + [hbm()] * 5,
        out_specs=[vmem()] * 7,
        scratch_shapes=[
            pltpu.VMEM(pool_index.shape, jnp.int32),
            pltpu.VMEM(act_scale.shape, jnp.float32),
            pltpu.VMEM(ids.shape, jnp.int32),
            pltpu.VMEM((act_scale.shape[1], 1), jnp.float32),
            pltpu.SemaphoreType.DMA((3,)),
            pltpu.SemaphoreType.DMA((3 + 2 * count,)),
        ],
        compiler_params=pltpu.CompilerParams(vmem_limit_bytes=4 * MIB),
        cost_estimate=pl.CostEstimate(
            flops=0, bytes_accessed=4 * count * kb * gl.shape[1], transcendentals=0
        ),
        name="fill",
    )(where, pool_index, act_scale, ids, gl, gs, ul, us, ds)


def run(steps, stage, ahead):
    for c in ahead:
        c.start()

    def body(step, carry):
        stage(step)
        return carry

    lax.fori_loop(0, steps, body, 0)
    for c in ahead:
        c.wait()


def gate_up_kernel(pieces, distances, coming, first, last, kb, ahead, where, *refs):
    blocks = len(distances)
    rows_in = refs[: pieces * blocks]
    refs = refs[pieces * blocks :]
    gl, gs, ul, us, g_held, u_held = refs[:6]
    refs = refs[6:]
    if not first:
        gate_in, up_in = refs[:2]
        refs = refs[2:]
    if last:
        act_scale, dl, hidden, d_next = refs[:4]
        refs = refs[4:]
        gate, up = refs[:2]
        refs = refs[2:]
    else:
        gate, up, g_next, u_next = refs[:4]
        refs = refs[4:]
    xs, row_sems, ahead_sems = refs
    rows = rows_in[0].shape[0]
    depth = rows_in[0].shape[1]
    per_block = depth // kb
    steps = blocks * per_block

    row_copies = [
        pltpu.make_async_copy(
            rows_in[b * pieces + p],
            xs.at[p * rows : (p + 1) * rows, b * depth : (b + 1) * depth],
            row_sems.at[b * pieces + p],
        )
        for b in range(blocks)
        for p in range(pieces)
    ]
    for c in row_copies:
        c.start()

    def place(step):
        block = where[1] ^ distances[0]
        for b in range(1, blocks):
            block = jnp.where(step // per_block == b, where[1] ^ distances[b], block)
        return pl.multiple_of(block * depth + (step % per_block) * kb, kb)

    following = []
    for j in range(ahead):
        if last:
            down_kb, width = d_next.shape[1:]
            col = pl.multiple_of((where[1] ^ coming[0]) * width, width)
            source = dl.at[j * down_kb : (j + 1) * down_kb, pl.ds(col, width)]
            following.append(pltpu.make_async_copy(source, d_next.at[j], ahead_sems.at[j]))
        else:
            k = (where[1] ^ coming[j // per_block]) * depth + (j % per_block) * kb
            k = pl.multiple_of(k, kb)
            for i, (a, b) in enumerate(((gl, g_next), (ul, u_next))):
                following.append(
                    pltpu.make_async_copy(
                        a.at[pl.ds(k, kb), :], b.at[j], ahead_sems.at[2 * j + i]
                    )
                )

    def add(total, given, scales, step):
        block = given.at[step]
        group = place(step) // GROUP
        total[...] += jnp.dot(
            xs[:, pl.ds(pl.multiple_of(step * kb, kb), kb)],
            scaled(block, scales, group, kb // GROUP),
            preferred_element_type=jnp.float32,
        )

    if first:
        gate[...] = jnp.zeros_like(gate)
        up[...] = jnp.zeros_like(up)
    else:
        gate[...] = gate_in[...]
        up[...] = up_in[...]
    for c in row_copies:
        c.wait()
    def both(step):
        add(gate, g_held, gs, step)
        add(up, u_held, us, step)

    run(steps, both, following)
    if last:
        g = gate[...] * act_scale[...]
        u = up[...] * act_scale[...]
        hidden[...] = (g / (1.0 + jnp.exp(-g)) * u).astype(jnp.bfloat16)


def gate_up(where, distances, coming, blocks_in, gl, gs, ul, us, carried, acc, act_scale, dl, kb, down_kb, ahead):
    first, last = acc is None, act_scale is not None
    blocks, pieces = len(blocks_in), len(blocks_in[0])
    rows, depth = blocks_in[0][0].shape
    width = gl.shape[1]
    ins = [where] + [p for b in blocks_in for p in b] + [gl, gs, ul, us] + list(carried)
    specs = [smem()] + [anywhere()] * (blocks * pieces) + [hbm(), vmem(), hbm(), vmem()]
    specs += [vmem(), vmem()]
    if not first:
        ins += list(acc)
        specs += [vmem(), vmem()]
    total = jax.ShapeDtypeStruct((rows * pieces, width), jnp.float32)
    scratch = []
    if last:
        ins += [act_scale, dl]
        specs += [vmem(), hbm()]
        out_shape = [jax.ShapeDtypeStruct((rows * pieces, width), jnp.bfloat16)]
        out_shape += [pltpu.VMEM((ahead, down_kb, depth), jnp.bfloat16)]
        scratch += [pltpu.VMEM(total.shape, jnp.float32)] * 2
    else:
        out_shape = [total, total] + [pltpu.VMEM((ahead, kb, width), jnp.bfloat16)] * 2
    scratch += [
        pltpu.VMEM((rows * pieces, blocks * depth), jnp.bfloat16),
        pltpu.SemaphoreType.DMA((blocks * pieces,)),
        pltpu.SemaphoreType.DMA((2 * ahead,)),
    ]
    return pl.pallas_call(
        functools.partial(gate_up_kernel, pieces, distances, coming, first, last, kb, ahead),
        out_shape=out_shape,
        in_specs=specs,
        out_specs=[vmem()] * len(out_shape),
        scratch_shapes=scratch,
        compiler_params=pltpu.CompilerParams(vmem_limit_bytes=8 * MIB),
        cost_estimate=pl.CostEstimate(
            flops=4 * rows * pieces * blocks * depth * width,
            bytes_accessed=4 * blocks * depth * width,
            transcendentals=0,
        ),
        name="gate_up",
    )(*ins)


def down_kernel(distances, kb, ahead, shrink_too, where, hidden, dl, ds, d_held, *refs):
    if shrink_too:
        shrink = refs[0]
        refs = refs[1:]
    mine, theirs = refs[:2]
    refs = refs[2:]
    if ahead:
        d_next = refs[0]
        refs = refs[1:]
    acc, ahead_sems = refs
    depth, width = hidden.shape[1], acc.shape[1]
    half = mine.shape[0]
    steps = depth // kb
    col = pl.multiple_of((where[1] ^ distances[0]) * width, width)

    following = []
    for j in range(ahead):
        next_col = pl.multiple_of((where[1] ^ distances[1]) * width, width)
        source = dl.at[j * kb : (j + 1) * kb, pl.ds(next_col, width)]
        following.append(pltpu.make_async_copy(source, d_next.at[j], ahead_sems.at[j]))

    def add(step):
        block = d_held.at[step]
        parts = []
        for g in range(kb // GROUP):
            row = ds[pl.ds(step * (kb // GROUP) + g, 1), pl.ds(col, width)].astype(jnp.bfloat16)
            parts.append(block[g * GROUP : (g + 1) * GROUP, :] * row)
        weight = jnp.concatenate(parts, axis=0) if len(parts) > 1 else parts[0]
        acc[...] += jnp.dot(
            hidden[:, pl.ds(pl.multiple_of(step * kb, kb), kb)],
            weight,
            preferred_element_type=jnp.float32,
        )

    def project():
        low = jnp.dot(hidden[...], shrink[...], preferred_element_type=jnp.float32)
        mine[:, width:] = low[:half]
        theirs[:, width:] = low[half:].astype(jnp.bfloat16)

    acc[...] = jnp.zeros_like(acc)
    run(steps, add, following)
    if shrink_too:
        project()
    mine[:, :width] = acc[:half, :]
    theirs[:, :width] = acc[half:, :].astype(jnp.bfloat16)


def down(where, distances, hidden, dl, ds, carried, width, shrink, kb, ahead):
    rows, depth = hidden.shape
    wide = width + (0 if shrink is None else shrink.shape[1])
    ins = [where, hidden, dl, ds, carried]
    specs = [smem(), vmem(), hbm(), vmem(), vmem()]
    if shrink is not None:
        ins.append(shrink)
        specs.append(vmem())
    out_shape = [
        jax.ShapeDtypeStruct((rows // 2, wide), jnp.float32),
        jax.ShapeDtypeStruct((rows // 2, wide), jnp.bfloat16),
    ]
    if ahead:
        out_shape.append(pltpu.VMEM((ahead, kb, width), jnp.bfloat16))
    return pl.pallas_call(
        functools.partial(down_kernel, distances, kb, ahead, shrink is not None),
        out_shape=out_shape,
        in_specs=specs,
        out_specs=[vmem()] * len(out_shape),
        scratch_shapes=[
            pltpu.VMEM((rows, width), jnp.float32),
            pltpu.SemaphoreType.DMA((max(1, ahead),)),
        ],
        compiler_params=pltpu.CompilerParams(vmem_limit_bytes=8 * MIB),
        cost_estimate=pl.CostEstimate(
            flops=2 * rows * depth * width, bytes_accessed=2 * depth * width, transcendentals=0
        ),
        name="down",
    )(*ins)


def cost(count):
    return pl.CostEstimate(flops=count, bytes_accessed=4 * count, transcendentals=0)


def pair_kernel(chips, mine, got, own, *send):
    rows = own.shape[0]
    own[...] = mine[:rows, :] + got[:rows, :].astype(jnp.float32)
    for s in range(1, chips):
        at = slice(s * rows, (s + 1) * rows)
        send[s - 1][...] = (mine[at, :] + got[at, :].astype(jnp.float32)).astype(jnp.bfloat16)


def pair_sum(mine, got, chips):
    rows, width = mine.shape[0] // chips, mine.shape[1]
    out_shape = [jax.ShapeDtypeStruct((rows, width), jnp.float32)]
    out_shape += [jax.ShapeDtypeStruct((rows, width), jnp.bfloat16)] * (chips - 1)
    return pl.pallas_call(
        functools.partial(pair_kernel, chips),
        out_shape=out_shape,
        in_specs=[vmem()] * 2,
        out_specs=[vmem()] * chips,
        compiler_params=pltpu.CompilerParams(vmem_limit_bytes=4 * MIB),
        cost_estimate=cost(rows * chips * width),
        name="pair",
    )(mine, got)


def attach_kernel(count, low, *refs):
    parts, out = refs[:count], refs[count]
    width = parts[0].shape[1]
    total = parts[0][...]
    for p in parts[1:]:
        total = total + p[...].astype(jnp.float32)
    out[:, :width] = total.astype(jnp.bfloat16)
    out[:, width:] = low[...]


def attach(parts, low):
    rows, width = parts[0].shape
    return pl.pallas_call(
        functools.partial(attach_kernel, len(parts)),
        out_shape=jax.ShapeDtypeStruct((rows, width + low.shape[1]), jnp.bfloat16),
        in_specs=[vmem()] * (1 + len(parts)),
        out_specs=vmem(),
        compiler_params=pltpu.CompilerParams(vmem_limit_bytes=4 * MIB),
        cost_estimate=cost(rows * width * len(parts)),
        name="attach",
    )(low, *parts)


def fold_matrix(pool_width, rank, lanes, transposed):
    shape = (lanes, pool_width) if transposed else (pool_width, lanes)
    wide = lax.broadcasted_iota(jnp.int32, shape, 1 if transposed else 0)
    slim = lax.broadcasted_iota(jnp.int32, shape, 0 if transposed else 1)
    return (lax.rem(wide, rank) == slim).astype(jnp.float32).astype(jnp.bfloat16)


def pool_mask(pool_row, rows, pool_width, rank):
    column = lax.broadcasted_iota(jnp.int32, (rows, pool_width), 1)
    start = pool_row * rank
    return (column >= start) & (column < start + rank)


def message_kernel(count, width, rank, pool_row, *refs):
    parts, (out, low) = refs[:count], refs[count:]
    total = parts[0][...].astype(jnp.float32)
    for p in parts[1:]:
        total = total + p[...].astype(jnp.float32)
    rows, wide = total.shape
    mask = pool_mask(pool_row[...], rows, wide - width, rank)
    chosen = jnp.where(mask, total[:, width:], 0.0).astype(jnp.bfloat16)
    part = jnp.dot(
        chosen,
        fold_matrix(wide - width, rank, low.shape[1], False),
        preferred_element_type=jnp.float32,
    ).astype(jnp.bfloat16)
    low[...] = part
    out[:, :width] = total[:, :width].astype(jnp.bfloat16)
    out[:, width:] = part


def message(parts, pool_row, width, rank):
    rows = parts[0].shape[0]
    lanes = max(LANES, rank)
    return pl.pallas_call(
        functools.partial(message_kernel, len(parts), width, rank),
        out_shape=[
            jax.ShapeDtypeStruct((rows, width + lanes), jnp.bfloat16),
            jax.ShapeDtypeStruct((rows, lanes), jnp.bfloat16),
        ],
        in_specs=[vmem()] * (1 + len(parts)),
        out_specs=[vmem()] * 2,
        compiler_params=pltpu.CompilerParams(vmem_limit_bytes=6 * MIB),
        cost_estimate=cost(rows * width * len(parts)),
        name="message",
    )(pool_row, *parts)


def final_kernel(count, wides, order, rank, where, pool_row, low, *refs):
    pieces = len(order)
    pool, refs = refs[:pieces], refs[pieces:]
    parts, wide, out = refs[:count], refs[count : count + wides], refs[count + wides]
    rows, width = out.shape
    total_low = low[...].astype(jnp.float32)
    for w in wide:
        total_low = total_low + w[:, width:].astype(jnp.float32)
    total_low = total_low.astype(jnp.bfloat16)
    pool_width = pool[0].shape[0]
    spread = jnp.dot(
        total_low,
        fold_matrix(pool_width, rank, total_low.shape[1], True),
        preferred_element_type=jnp.float32,
    )
    total = jnp.zeros((rows, width), jnp.float32)
    for p in range(pieces):
        held = pool_row[...] - (where[0] ^ order[p]) * (pool_width // rank)
        mask = pool_mask(held, rows, pool_width, rank)
        chosen = jnp.where(mask, spread, 0.0).astype(jnp.bfloat16)
        total = total + jnp.dot(chosen, pool[p][...], preferred_element_type=jnp.float32)
    for p in parts:
        total = total + p[...].astype(jnp.float32)
    for w in wide:
        total = total + w[:, :width].astype(jnp.float32)
    out[...] = total.astype(jnp.bfloat16)


def final(parts, wide, where, order, pool_row, low, pool, rank):
    rows, width = parts[0].shape
    return pl.pallas_call(
        functools.partial(final_kernel, len(parts), len(wide), order, rank),
        out_shape=jax.ShapeDtypeStruct((rows, width), jnp.bfloat16),
        in_specs=[smem()] + [vmem()] * (2 + len(pool) + len(parts) + len(wide)),
        out_specs=vmem(),
        compiler_params=pltpu.CompilerParams(vmem_limit_bytes=4 * MIB),
        name="final",
            cost_estimate=cost(0),
    )(where, pool_row, low, *pool, *parts, *wide)


def nearest_first(count):
    return sorted(range(1, count), key=lambda d: (d.bit_length(), -d))


def local(replicas, tensors, *args):
    (
        act_codes,
        act_scale,
        adapter_ids,
        seg_starts,
        pool_index,
        gate_levels,
        gate_scale,
        up_levels,
        up_scale,
        down_levels,
        down_scale,
        shrink_weight,
        expand_rows,
    ) = args
    replica = lax.axis_index("replica")
    tensor = lax.axis_index("tensor")
    cores = 2
    chips = replicas // cores
    rows, depth = act_codes.shape
    rank, width = expand_rows.shape[1], expand_rows.shape[2]
    hidden_rows = down_levels.shape[0]

    def core_swap(v):
        return lax.ppermute(v, "replica", [(r, r ^ 1) for r in range(replicas)])

    def chip_swap(v, s):
        return lax.ppermute(v, "replica", [(r, r ^ (s * cores)) for r in range(replicas)])

    def tensor_swap(v, d):
        return lax.ppermute(v, "tensor", [(t, t ^ d) for t in range(tensors)])

    order = [s * cores for s in range(chips)] + [s * cores + 1 for s in range(chips)]

    def spread_block(v):
        same = [v] + [chip_swap(v, s) for s in range(1, chips)]
        return same + [core_swap(p) for p in same]

    gate_levels, up_levels, down_levels, gate_scale, up_scale, down_scale = (
        pltpu.with_memory_space_constraint(v, pltpu.HBM)
        for v in (gate_levels, up_levels, down_levels, gate_scale, up_scale, down_scale)
    )
    near = [0] + nearest_first(tensors)
    far = near[1:][::-1] + [0]
    kb = min(BLOCK, depth)
    down_kb = min(BLOCK, hidden_rows)
    where = jnp.stack([replica, tensor]).astype(jnp.int32)

    groups = [near[:1]]
    rest = near[1:]
    if len(rest) <= 3:
        groups += [[d] for d in rest]
    else:
        groups += [rest[: len(rest) // 2], rest[len(rest) // 2 :]]

    moved = {d: tensor_swap(act_codes, d) for d in groups[1]}
    same = [act_codes] + [chip_swap(act_codes, s) for s in range(1, chips)]
    filled = fill(
        where,
        *(
            pltpu.with_memory_space_constraint(v[None, :], pltpu.HBM)
            for v in (pool_index, act_scale, adapter_ids)
        ),
        order,
        depth,
        gate_levels,
        gate_scale,
        up_levels,
        up_scale,
        down_scale,
        kb,
        depth // kb,
    )
    carried = filled[:2]
    gate_scale, up_scale, down_scale, row_scale, pool_row = filled[2:]
    arrived = {0: same + [core_swap(after(p, pool_row)) for p in same]}
    codes_later = after(act_codes, pool_row)
    for d in groups[1]:
        arrived[d] = spread_block(after(moved[d], pool_row))
    for late in groups[2:]:
        for d in late:
            moved[d] = tensor_swap(codes_later, d)
    acc = None
    for i, g in enumerate(groups):
        is_last = i == len(groups) - 1
        following = far[:1] if is_last else groups[i + 1]
        out = gate_up(
            where,
            g,
            following,
            [arrived[d] for d in g],
            gate_levels,
            gate_scale,
            up_levels,
            up_scale,
            carried,
            acc,
            row_scale if is_last else None,
            down_levels,
            kb,
            down_kb,
            hidden_rows // down_kb if is_last else len(following) * depth // kb,
        )
        if is_last:
            hidden, carried = out
        else:
            acc, carried = out[:2], out[2:]
        if i == 0:
            for late in groups[2:]:
                for d in late:
                    arrived[d] = spread_block(after(moved[d], acc[0]))
        if i == 1:
            pool = spread_block(after(expand_rows.reshape(-1, width), acc[0]))

    low = None
    received = []
    sent, sums, messages = [], [], []
    for n, d in enumerate(far):
        more = n + 1 < len(far)
        source = hidden
        if n >= 2:
            source = after(source, sums[n - 2])
        if n >= 3:
            source = after(source, messages[n - 3])
        out = down(
            where,
            [d] + far[n + 1 : n + 2],
            source,
            down_levels,
            down_scale,
            carried,
            width,
            shrink_weight if n == 0 else None,
            down_kb,
            hidden_rows // down_kb if more else 0,
        )
        mine, theirs = out[:2]
        carried = out[2] if more else None
        got = core_swap(theirs)
        if not more:
            got = after(got, *messages, received[0])
        own, *send = pair_sum(mine, got, chips)
        sums.append(send[0])
        parts = [own] + [chip_swap(send[s - 1], s) for s in range(1, chips)]
        if n == 0:
            block, low = message(parts, pool_row, width, rank)
        elif d:
            block = attach(parts, low)
        if d:
            messages.append(block)
            received.append(tensor_swap(block, d))
    return final(parts, received, where, order, pool_row, low, pool, rank)


def solution(mesh):
    placed = (
        P(("parts", "replica"), "tensor"),
        P("parts"),
        P(("parts", "replica")),
        P("parts", None),
        P("parts"),
        P(None, ("replica", "tensor")),
        P(None, ("replica", "tensor")),
        P(None, ("replica", "tensor")),
        P(None, ("replica", "tensor")),
        P(("replica", "tensor"), None),
        P(("replica", "tensor"), None),
        P(("replica", "tensor"), None),
        P("replica", None, "tensor"),
    )
    return jax.shard_map(
        functools.partial(local, mesh.shape["replica"], mesh.shape["tensor"]),
        mesh=mesh,
        in_specs=placed,
        out_specs=P(("parts", "replica"), "tensor"),
        check_vma=False,
    )
```

```python
import functools
import jax
import jax.numpy as jnp
from jax import lax
from jax.experimental import pallas as pl
from jax.experimental.pallas import tpu as pltpu
from jax.sharding import PartitionSpec as P

GROUP = 128
LANES = 128
MIB = 1024 * 1024
BLOCK = 512


def vmem():
    return pl.BlockSpec(memory_space=pltpu.VMEM)


def smem():
    return pl.BlockSpec(memory_space=pltpu.SMEM)


def hbm():
    return pl.BlockSpec(memory_space=pltpu.HBM)


def anywhere():
    return pl.BlockSpec(memory_space=pl.ANY)


def after(value, *earlier):
    return lax.optimization_barrier((value,) + earlier)[0]


def scaled(levels, scales, first_group, groups):
    parts = []
    for g in range(groups):
        row = scales[pl.ds(first_group + g, 1), :].astype(jnp.bfloat16)
        parts.append(levels[g * GROUP : (g + 1) * GROUP, :] * row)
    return jnp.concatenate(parts, axis=0) if groups > 1 else parts[0]


def as_column(row):
    rows = row.shape[1]
    place = lax.broadcasted_iota(jnp.int32, (rows, rows), 0)
    same = place == lax.broadcasted_iota(jnp.int32, (rows, rows), 1)
    return jnp.sum(jnp.where(same, row, jnp.zeros_like(row)), axis=1, keepdims=True)


def fill_kernel(
    kb, count, depth, order, where, pool_index, act_scale, ids,
    gl, gs, ul, us, ds, gbuf, ubuf, gs_out, us_out, ds_out, row_scale, pool_row,
    pool_held, act_held, ids_held, act_column, small_sems, sems,
):
    k = pl.multiple_of(where[1] * depth, kb)
    small = [(pool_index, pool_held), (act_scale, act_held), (ids, ids_held)]
    small = [pltpu.make_async_copy(a, b, small_sems.at[i]) for i, (a, b) in enumerate(small)]
    for c in small:
        c.start()
    moves = [(gs, gs_out), (us, us_out), (ds, ds_out)]
    for j in range(count):
        rows = pl.ds(k + j * kb, kb)
        moves += [(gl.at[rows, :], gbuf.at[j]), (ul.at[rows, :], ubuf.at[j])]
    made = [pltpu.make_async_copy(a, b, sems.at[i]) for i, (a, b) in enumerate(moves)]
    for c in made:
        c.start()
    for c in small:
        c.wait()
    rows = ids.shape[1]
    act_column[...] = as_column(act_held[...])
    for p, o in enumerate(order):
        at = pl.multiple_of((where[0] ^ o) * rows, rows)
        row_scale[p * rows : (p + 1) * rows, :] = act_column[pl.ds(at, rows), :]
    column = as_column(ids_held[...].astype(jnp.float32)).astype(jnp.int32)
    named = lax.broadcasted_iota(jnp.int32, (rows, pool_held.shape[1]), 1) == column
    chosen = jnp.where(named, pool_held[...].astype(jnp.float32), 0.0)
    pool_row[...] = jnp.sum(chosen, axis=1, keepdims=True).astype(jnp.int32)
    for c in made:
        c.wait()


def fill(where, pool_index, act_scale, ids, order, depth, gl, gs, ul, us, ds, kb, count):
    block = pltpu.VMEM((count, kb, gl.shape[1]), gl.dtype)
    out_shape = [block, block] + [jax.ShapeDtypeStruct(v.shape, v.dtype) for v in (gs, us, ds)]
    rows = ids.shape[1]
    out_shape += [
        jax.ShapeDtypeStruct((rows * len(order), 1), jnp.float32),
        jax.ShapeDtypeStruct((rows, 1), jnp.int32),
    ]
    return pl.pallas_call(
        functools.partial(fill_kernel, kb, count, depth, order),
        out_shape=out_shape,
        in_specs=[smem()] + [anywhere()] * 3 + [hbm()] * 5,
        out_specs=[vmem()] * 7,
        scratch_shapes=[
            pltpu.VMEM(pool_index.shape, jnp.int32),
            pltpu.VMEM(act_scale.shape, jnp.float32),
            pltpu.VMEM(ids.shape, jnp.int32),
            pltpu.VMEM((act_scale.shape[1], 1), jnp.float32),
            pltpu.SemaphoreType.DMA((3,)),
            pltpu.SemaphoreType.DMA((3 + 2 * count,)),
        ],
        compiler_params=pltpu.CompilerParams(vmem_limit_bytes=4 * MIB),
        cost_estimate=pl.CostEstimate(
            flops=0, bytes_accessed=4 * count * kb * gl.shape[1], transcendentals=0
        ),
        name="fill",
    )(where, pool_index, act_scale, ids, gl, gs, ul, us, ds)


def run(steps, stage, ahead):
    def body(step, carry):
        stage(step)
        return carry

    lax.fori_loop(0, steps, body, 0)
    for c in ahead:
        c.wait()


def gate_up_kernel(pieces, distances, coming, first, last, kb, ahead, where, *refs):
    blocks = len(distances)
    rows_in = refs[: pieces * blocks]
    refs = refs[pieces * blocks :]
    gl, gs, ul, us, g_held, u_held = refs[:6]
    refs = refs[6:]
    if not first:
        gate_in, up_in = refs[:2]
        refs = refs[2:]
    if last:
        act_scale, dl, hidden, d_next = refs[:4]
        refs = refs[4:]
        gate, up = refs[:2]
        refs = refs[2:]
    else:
        gate, up, g_next, u_next = refs[:4]
        refs = refs[4:]
    xs, row_sems, ahead_sems = refs
    rows = rows_in[0].shape[0]
    depth = rows_in[0].shape[1]
    per_block = depth // kb
    steps = blocks * per_block

    row_copies = [
        pltpu.make_async_copy(
            rows_in[b * pieces + p],
            xs.at[p * rows : (p + 1) * rows, b * depth : (b + 1) * depth],
            row_sems.at[b * pieces + p],
        )
        for b in range(blocks)
        for p in range(pieces)
    ]
    for c in row_copies:
        c.start()

    def place(step):
        block = where[1] ^ distances[0]
        for b in range(1, blocks):
            block = jnp.where(step // per_block == b, where[1] ^ distances[b], block)
        return pl.multiple_of(block * depth + (step % per_block) * kb, kb)

    following = []
    for j in range(ahead):
        if last:
            down_kb, width = d_next.shape[1:]
            col = pl.multiple_of((where[1] ^ coming[0]) * width, width)
            source = dl.at[j * down_kb : (j + 1) * down_kb, pl.ds(col, width)]
            following.append(pltpu.make_async_copy(source, d_next.at[j], ahead_sems.at[j]))
        else:
            k = (where[1] ^ coming[j // per_block]) * depth + (j % per_block) * kb
            k = pl.multiple_of(k, kb)
            for i, (a, b) in enumerate(((gl, g_next), (ul, u_next))):
                following.append(
                    pltpu.make_async_copy(
                        a.at[pl.ds(k, kb), :], b.at[j], ahead_sems.at[2 * j + i]
                    )
                )

    def add(total, given, scales, step):
        block = given.at[step]
        group = place(step) // GROUP
        total[...] += jnp.dot(
            xs[:, pl.ds(pl.multiple_of(step * kb, kb), kb)],
            scaled(block, scales, group, kb // GROUP),
            preferred_element_type=jnp.float32,
        )

    for c in following:
        c.start()
    if first:
        gate[...] = jnp.zeros_like(gate)
        up[...] = jnp.zeros_like(up)
    else:
        gate[...] = gate_in[...]
        up[...] = up_in[...]
    for c in row_copies:
        c.wait()
    def both(step):
        add(gate, g_held, gs, step)
        add(up, u_held, us, step)

    run(steps, both, following)
    if last:
        g = gate[...] * act_scale[...]
        u = up[...] * act_scale[...]
        hidden[...] = (g / (1.0 + jnp.exp(-g)) * u).astype(jnp.bfloat16)


def gate_up(where, distances, coming, blocks_in, gl, gs, ul, us, carried, acc, act_scale, dl, kb, down_kb, ahead):
    first, last = acc is None, act_scale is not None
    blocks, pieces = len(blocks_in), len(blocks_in[0])
    rows, depth = blocks_in[0][0].shape
    width = gl.shape[1]
    ins = [where] + [p for b in blocks_in for p in b] + [gl, gs, ul, us] + list(carried)
    specs = [smem()] + [anywhere()] * (blocks * pieces) + [hbm(), vmem(), hbm(), vmem()]
    specs += [vmem(), vmem()]
    if not first:
        ins += list(acc)
        specs += [vmem(), vmem()]
    total = jax.ShapeDtypeStruct((rows * pieces, width), jnp.float32)
    scratch = []
    if last:
        ins += [act_scale, dl]
        specs += [vmem(), hbm()]
        out_shape = [jax.ShapeDtypeStruct((rows * pieces, width), jnp.bfloat16)]
        out_shape += [pltpu.VMEM((ahead, down_kb, depth), jnp.bfloat16)]
        scratch += [pltpu.VMEM(total.shape, jnp.float32)] * 2
    else:
        out_shape = [total, total] + [pltpu.VMEM((ahead, kb, width), jnp.bfloat16)] * 2
    scratch += [
        pltpu.VMEM((rows * pieces, blocks * depth), jnp.bfloat16),
        pltpu.SemaphoreType.DMA((blocks * pieces,)),
        pltpu.SemaphoreType.DMA((2 * ahead,)),
    ]
    return pl.pallas_call(
        functools.partial(gate_up_kernel, pieces, distances, coming, first, last, kb, ahead),
        out_shape=out_shape,
        in_specs=specs,
        out_specs=[vmem()] * len(out_shape),
        scratch_shapes=scratch,
        compiler_params=pltpu.CompilerParams(vmem_limit_bytes=8 * MIB),
        cost_estimate=pl.CostEstimate(
            flops=4 * rows * pieces * blocks * depth * width,
            bytes_accessed=4 * blocks * depth * width,
            transcendentals=0,
        ),
        name="gate_up",
    )(*ins)


def down_kernel(distances, kb, ahead, shrink_too, where, hidden, dl, ds, d_held, *refs):
    if shrink_too:
        shrink = refs[0]
        refs = refs[1:]
    mine, theirs = refs[:2]
    refs = refs[2:]
    if ahead:
        d_next = refs[0]
        refs = refs[1:]
    acc, ahead_sems = refs
    depth, width = hidden.shape[1], acc.shape[1]
    half = mine.shape[0]
    steps = depth // kb
    col = pl.multiple_of((where[1] ^ distances[0]) * width, width)

    following = []
    for j in range(ahead):
        next_col = pl.multiple_of((where[1] ^ distances[1]) * width, width)
        source = dl.at[j * kb : (j + 1) * kb, pl.ds(next_col, width)]
        following.append(pltpu.make_async_copy(source, d_next.at[j], ahead_sems.at[j]))

    def add(step):
        block = d_held.at[step]
        parts = []
        for g in range(kb // GROUP):
            row = ds[pl.ds(step * (kb // GROUP) + g, 1), pl.ds(col, width)].astype(jnp.bfloat16)
            parts.append(block[g * GROUP : (g + 1) * GROUP, :] * row)
        weight = jnp.concatenate(parts, axis=0) if len(parts) > 1 else parts[0]
        acc[...] += jnp.dot(
            hidden[:, pl.ds(pl.multiple_of(step * kb, kb), kb)],
            weight,
            preferred_element_type=jnp.float32,
        )

    def project():
        low = jnp.dot(hidden[...], shrink[...], preferred_element_type=jnp.float32)
        mine[:, width:] = low[:half]
        theirs[:, width:] = low[half:].astype(jnp.bfloat16)

    for c in following:
        c.start()
    acc[...] = jnp.zeros_like(acc)
    run(steps, add, following)
    if shrink_too:
        project()
    mine[:, :width] = acc[:half, :]
    theirs[:, :width] = acc[half:, :].astype(jnp.bfloat16)


def down(where, distances, hidden, dl, ds, carried, width, shrink, kb, ahead):
    rows, depth = hidden.shape
    wide = width + (0 if shrink is None else shrink.shape[1])
    ins = [where, hidden, dl, ds, carried]
    specs = [smem(), vmem(), hbm(), vmem(), vmem()]
    if shrink is not None:
        ins.append(shrink)
        specs.append(vmem())
    out_shape = [
        jax.ShapeDtypeStruct((rows // 2, wide), jnp.float32),
        jax.ShapeDtypeStruct((rows // 2, wide), jnp.bfloat16),
    ]
    if ahead:
        out_shape.append(pltpu.VMEM((ahead, kb, width), jnp.bfloat16))
    return pl.pallas_call(
        functools.partial(down_kernel, distances, kb, ahead, shrink is not None),
        out_shape=out_shape,
        in_specs=specs,
        out_specs=[vmem()] * len(out_shape),
        scratch_shapes=[
            pltpu.VMEM((rows, width), jnp.float32),
            pltpu.SemaphoreType.DMA((max(1, ahead),)),
        ],
        compiler_params=pltpu.CompilerParams(vmem_limit_bytes=8 * MIB),
        cost_estimate=pl.CostEstimate(
            flops=2 * rows * depth * width, bytes_accessed=2 * depth * width, transcendentals=0
        ),
        name="down",
    )(*ins)


def cost(count):
    return pl.CostEstimate(flops=count, bytes_accessed=4 * count, transcendentals=0)


def pair_kernel(chips, mine, got, own, *send):
    rows = own.shape[0]
    own[...] = mine[:rows, :] + got[:rows, :].astype(jnp.float32)
    for s in range(1, chips):
        at = slice(s * rows, (s + 1) * rows)
        send[s - 1][...] = (mine[at, :] + got[at, :].astype(jnp.float32)).astype(jnp.bfloat16)


def pair_sum(mine, got, chips):
    rows, width = mine.shape[0] // chips, mine.shape[1]
    out_shape = [jax.ShapeDtypeStruct((rows, width), jnp.float32)]
    out_shape += [jax.ShapeDtypeStruct((rows, width), jnp.bfloat16)] * (chips - 1)
    return pl.pallas_call(
        functools.partial(pair_kernel, chips),
        out_shape=out_shape,
        in_specs=[vmem()] * 2,
        out_specs=[vmem()] * chips,
        compiler_params=pltpu.CompilerParams(vmem_limit_bytes=4 * MIB),
        cost_estimate=cost(rows * chips * width),
        name="pair",
    )(mine, got)


def attach_kernel(count, low, *refs):
    parts, out = refs[:count], refs[count]
    width = parts[0].shape[1]
    total = parts[0][...]
    for p in parts[1:]:
        total = total + p[...].astype(jnp.float32)
    out[:, :width] = total.astype(jnp.bfloat16)
    out[:, width:] = low[...]


def attach(parts, low):
    rows, width = parts[0].shape
    return pl.pallas_call(
        functools.partial(attach_kernel, len(parts)),
        out_shape=jax.ShapeDtypeStruct((rows, width + low.shape[1]), jnp.bfloat16),
        in_specs=[vmem()] * (1 + len(parts)),
        out_specs=vmem(),
        compiler_params=pltpu.CompilerParams(vmem_limit_bytes=4 * MIB),
        cost_estimate=cost(rows * width * len(parts)),
        name="attach",
    )(low, *parts)


def fold_matrix(pool_width, rank, lanes, transposed):
    shape = (lanes, pool_width) if transposed else (pool_width, lanes)
    wide = lax.broadcasted_iota(jnp.int32, shape, 1 if transposed else 0)
    slim = lax.broadcasted_iota(jnp.int32, shape, 0 if transposed else 1)
    return (lax.rem(wide, rank) == slim).astype(jnp.float32).astype(jnp.bfloat16)


def pool_mask(pool_row, rows, pool_width, rank):
    column = lax.broadcasted_iota(jnp.int32, (rows, pool_width), 1)
    start = pool_row * rank
    return (column >= start) & (column < start + rank)


def message_kernel(count, width, rank, pool_row, *refs):
    parts, (out, low) = refs[:count], refs[count:]
    total = parts[0][...].astype(jnp.float32)
    for p in parts[1:]:
        total = total + p[...].astype(jnp.float32)
    rows, wide = total.shape
    mask = pool_mask(pool_row[...], rows, wide - width, rank)
    chosen = jnp.where(mask, total[:, width:], 0.0).astype(jnp.bfloat16)
    part = jnp.dot(
        chosen,
        fold_matrix(wide - width, rank, low.shape[1], False),
        preferred_element_type=jnp.float32,
    ).astype(jnp.bfloat16)
    low[...] = part
    out[:, :width] = total[:, :width].astype(jnp.bfloat16)
    out[:, width:] = part


def message(parts, pool_row, width, rank):
    rows = parts[0].shape[0]
    lanes = max(LANES, rank)
    return pl.pallas_call(
        functools.partial(message_kernel, len(parts), width, rank),
        out_shape=[
            jax.ShapeDtypeStruct((rows, width + lanes), jnp.bfloat16),
            jax.ShapeDtypeStruct((rows, lanes), jnp.bfloat16),
        ],
        in_specs=[vmem()] * (1 + len(parts)),
        out_specs=[vmem()] * 2,
        compiler_params=pltpu.CompilerParams(vmem_limit_bytes=6 * MIB),
        cost_estimate=cost(rows * width * len(parts)),
        name="message",
    )(pool_row, *parts)


def final_kernel(count, wides, order, rank, where, pool_row, low, *refs):
    pieces = len(order)
    pool, refs = refs[:pieces], refs[pieces:]
    parts, wide, out = refs[:count], refs[count : count + wides], refs[count + wides]
    rows, width = out.shape
    total_low = low[...].astype(jnp.float32)
    for w in wide:
        total_low = total_low + w[:, width:].astype(jnp.float32)
    total_low = total_low.astype(jnp.bfloat16)
    pool_width = pool[0].shape[0]
    spread = jnp.dot(
        total_low,
        fold_matrix(pool_width, rank, total_low.shape[1], True),
        preferred_element_type=jnp.float32,
    )
    total = jnp.zeros((rows, width), jnp.float32)
    for p in range(pieces):
        held = pool_row[...] - (where[0] ^ order[p]) * (pool_width // rank)
        mask = pool_mask(held, rows, pool_width, rank)
        chosen = jnp.where(mask, spread, 0.0).astype(jnp.bfloat16)
        total = total + jnp.dot(chosen, pool[p][...], preferred_element_type=jnp.float32)
    for p in parts:
        total = total + p[...].astype(jnp.float32)
    for w in wide:
        total = total + w[:, :width].astype(jnp.float32)
    out[...] = total.astype(jnp.bfloat16)


def final(parts, wide, where, order, pool_row, low, pool, rank):
    rows, width = parts[0].shape
    return pl.pallas_call(
        functools.partial(final_kernel, len(parts), len(wide), order, rank),
        out_shape=jax.ShapeDtypeStruct((rows, width), jnp.bfloat16),
        in_specs=[smem()] + [vmem()] * (2 + len(pool) + len(parts) + len(wide)),
        out_specs=vmem(),
        compiler_params=pltpu.CompilerParams(vmem_limit_bytes=4 * MIB),
        name="final",
            cost_estimate=cost(0),
    )(where, pool_row, low, *pool, *parts, *wide)


def nearest_first(count):
    return sorted(range(1, count), key=lambda d: (d.bit_length(), -d))


def local(replicas, tensors, *args):
    (
        act_codes,
        act_scale,
        adapter_ids,
        seg_starts,
        pool_index,
        gate_levels,
        gate_scale,
        up_levels,
        up_scale,
        down_levels,
        down_scale,
        shrink_weight,
        expand_rows,
    ) = args
    replica = lax.axis_index("replica")
    tensor = lax.axis_index("tensor")
    cores = 2
    chips = replicas // cores
    rows, depth = act_codes.shape
    rank, width = expand_rows.shape[1], expand_rows.shape[2]
    hidden_rows = down_levels.shape[0]

    def core_swap(v):
        return lax.ppermute(v, "replica", [(r, r ^ 1) for r in range(replicas)])

    def chip_swap(v, s):
        return lax.ppermute(v, "replica", [(r, r ^ (s * cores)) for r in range(replicas)])

    def tensor_swap(v, d):
        return lax.ppermute(v, "tensor", [(t, t ^ d) for t in range(tensors)])

    order = [s * cores for s in range(chips)] + [s * cores + 1 for s in range(chips)]

    def spread_block(v):
        same = [v] + [chip_swap(v, s) for s in range(1, chips)]
        return same + [core_swap(p) for p in same]

    gate_levels, up_levels, down_levels, gate_scale, up_scale, down_scale = (
        pltpu.with_memory_space_constraint(v, pltpu.HBM)
        for v in (gate_levels, up_levels, down_levels, gate_scale, up_scale, down_scale)
    )
    near = [0] + nearest_first(tensors)
    far = near[1:][::-1] + [0]
    kb = min(BLOCK, depth)
    down_kb = min(BLOCK, hidden_rows)
    where = jnp.stack([replica, tensor]).astype(jnp.int32)

    groups = [near[:1]]
    rest = near[1:]
    if len(rest) <= 3:
        groups += [[d] for d in rest]
    else:
        groups += [rest[: len(rest) // 2], rest[len(rest) // 2 :]]

    moved = {d: tensor_swap(act_codes, d) for d in groups[1]}
    same = [act_codes] + [chip_swap(act_codes, s) for s in range(1, chips)]
    filled = fill(
        where,
        *(
            pltpu.with_memory_space_constraint(v[None, :], pltpu.HBM)
            for v in (pool_index, act_scale, adapter_ids)
        ),
        order,
        depth,
        gate_levels,
        gate_scale,
        up_levels,
        up_scale,
        down_scale,
        kb,
        depth // kb,
    )
    carried = filled[:2]
    gate_scale, up_scale, down_scale, row_scale, pool_row = filled[2:]
    arrived = {0: same + [core_swap(after(p, pool_row)) for p in same]}
    codes_later = after(act_codes, pool_row)
    for d in groups[1]:
        arrived[d] = spread_block(after(moved[d], pool_row))
    for late in groups[2:]:
        for d in late:
            moved[d] = tensor_swap(codes_later, d)
    acc = None
    for i, g in enumerate(groups):
        is_last = i == len(groups) - 1
        following = far[:1] if is_last else groups[i + 1]
        out = gate_up(
            where,
            g,
            following,
            [arrived[d] for d in g],
            gate_levels,
            gate_scale,
            up_levels,
            up_scale,
            carried,
            acc,
            row_scale if is_last else None,
            down_levels,
            kb,
            down_kb,
            hidden_rows // down_kb if is_last else len(following) * depth // kb,
        )
        if is_last:
            hidden, carried = out
        else:
            acc, carried = out[:2], out[2:]
        if i == 0:
            for late in groups[2:]:
                for d in late:
                    arrived[d] = spread_block(after(moved[d], acc[0]))
        if i == 1:
            pool = spread_block(after(expand_rows.reshape(-1, width), acc[0]))

    low = None
    received = []
    sent, sums, messages = [], [], []
    for n, d in enumerate(far):
        more = n + 1 < len(far)
        source = hidden
        if n >= 2:
            source = after(source, sums[n - 2])
        if n >= 3:
            source = after(source, messages[n - 3])
        out = down(
            where,
            [d] + far[n + 1 : n + 2],
            source,
            down_levels,
            down_scale,
            carried,
            width,
            shrink_weight if n == 0 else None,
            down_kb,
            hidden_rows // down_kb if more else 0,
        )
        mine, theirs = out[:2]
        carried = out[2] if more else None
        got = core_swap(theirs)
        if not more:
            got = after(got, *messages, received[0])
        own, *send = pair_sum(mine, got, chips)
        sums.append(send[0])
        parts = [own] + [chip_swap(send[s - 1], s) for s in range(1, chips)]
        if n == 0:
            block, low = message(parts, pool_row, width, rank)
        elif d:
            block = attach(parts, low)
        if d:
            messages.append(block)
            received.append(tensor_swap(block, d))
    return final(parts, received, where, order, pool_row, low, pool, rank)


def solution(mesh):
    placed = (
        P(("parts", "replica"), "tensor"),
        P("parts"),
        P(("parts", "replica")),
        P("parts", None),
        P("parts"),
        P(None, ("replica", "tensor")),
        P(None, ("replica", "tensor")),
        P(None, ("replica", "tensor")),
        P(None, ("replica", "tensor")),
        P(("replica", "tensor"), None),
        P(("replica", "tensor"), None),
        P(("replica", "tensor"), None),
        P("replica", None, "tensor"),
    )
    return jax.shard_map(
        functools.partial(local, mesh.shape["replica"], mesh.shape["tensor"]),
        mesh=mesh,
        in_specs=placed,
        out_specs=P(("parts", "replica"), "tensor"),
        check_vma=False,
    )
```
